256 devices in a mesh: dp: 32 (over x, y, core), ctx: 8 (over z).
Axes of the slice: x: 4, y: 4, z: 8, core: 2. Of those that a mesh axis runs over, the one named last changes fastest.
Arguments:
- queries: bfloat16 [32, 2048, 1024], P('dp', 'ctx'), may hold values from -6 to 6
- keys: bfloat16 [32, 2048, 1024], P('dp', 'ctx'), may hold values from -6 to 6
- values: bfloat16 [32, 2048, 1024], P('dp', 'ctx'), may hold values from -6 to 6
- gates: bfloat16 [32, 2048, 1024], P('dp', 'ctx'), may hold values from -6 to 6
- cotangent: bfloat16 [32, 2048, 1024], P('dp', 'ctx'), may hold values from -6 to 6
- out_weight: bfloat16 [1024, 1024], replicated, may hold values from -0.1875 to 0.1875
- position_bias: float32 [8, 128], replicated, may hold values from -4 to 4
- distance_bucket: int32 [768], replicated, may hold values from 0 to 127, as said below
- history_lengths: int32 [32, 8], P('dp'), may hold values from 0 to 768, as said below
- first_device: int32 [32], P('dp'), may hold values from 0 to 7
Outputs:
- d_queries: bfloat16 [32, 2048, 1024], P('dp', 'ctx')
- d_keys: bfloat16 [32, 2048, 1024], P('dp', 'ctx')
- d_values: bfloat16 [32, 2048, 1024], P('dp', 'ctx')
- d_gates: bfloat16 [32, 2048, 1024], P('dp', 'ctx')
- d_out_weight: float32 [1024, 1024], P('dp', 'ctx')
The draws below stay inside these ranges and needn't reach their ends.
Inputs may be any that keep to these rules, and one draw needn't show every extreme that they name: `distance_bucket`: Non-decreasing in the distance, 0 at distance 0, rising by at most 1 from one distance to the next. `history_lengths`: in each group the users' block counts ceil(length / 256) are 1 to 3 and sum to 8; entries after the last user are 0; every group has a user of exactly 768 events.
All inputs are finite; a program needn't handle non-finite values.
Results may differ from the reference program's by a relative error of at most 0.025.
Values may be sent and summed in bfloat16 or wider, within the bound.
A program may use at most 128 MiB of HBM per device.

```python
import jax
import jax.numpy as jnp
from jax import lax

D = 1024
HEADS = 8
NBUCK = 128
BLK = 256
MAXB = 3
ROWS = 2048
N_DP = 32
N_CTX = 8


def draw_history_lengths(key, part):
    key = jax.random.fold_in(key, 11)
    first_key, second_key, third_key = jax.random.split(key, 3)
    group_count = N_DP
    slot_count = N_CTX
    leftover = slot_count - MAXB
    counts = jax.random.randint(first_key, (group_count, slot_count), 1, MAXB + 1)
    block_ends = jnp.cumsum(counts, axis=1).astype(jnp.int32)
    block_starts = block_ends - counts
    taken = block_starts < leftover
    counts = jnp.where(taken, jnp.minimum(counts, leftover - block_starts), 0)
    user_count = jnp.sum(taken.astype(jnp.int32), axis=1, keepdims=True)
    placed = jax.random.randint(second_key, (group_count, 1), 0, 1 << 20) % (user_count + 1)
    slot_index = jnp.arange(slot_count, dtype=jnp.int32)[None, :]
    shifted = jnp.concatenate([jnp.zeros((group_count, 1), jnp.int32), counts[:, :-1]], axis=1)
    blocks_per = jnp.where(slot_index < placed, counts, jnp.where(slot_index == placed, MAXB, shifted))
    extra = jax.random.randint(third_key, (group_count, slot_count), 1, BLK + 1)
    lengths = jnp.where(blocks_per > 0, (blocks_per - 1) * BLK + extra, 0)
    lengths = jnp.where(slot_index == placed, MAXB * BLK, lengths)
    return lengths.astype(jnp.int32)


def draw_distance_bucket(key, part):
    key = jax.random.fold_in(key, 23)
    shuffled = jax.random.permutation(key, MAXB * BLK - 1)
    rises = jnp.zeros((MAXB * BLK,), jnp.int32).at[shuffled[:NBUCK - 1] + 1].set(1)
    return jnp.cumsum(rises).astype(jnp.int32)


def with_ends(array, own_key, low, largest):
    longest = array.shape.index(max(array.shape))
    spots = []
    for shift in (0, 1):
        where = [jax.random.randint(jax.random.fold_in(own_key, axis), (), 0, length) for axis, length in enumerate(array.shape)]
        where[longest] = (where[longest] + shift) % array.shape[longest]
        spots.append(tuple(where))
    return array.at[spots[0]].set(low).at[spots[1]].set(largest)


def raised(drawn, rng, source, target, blocks, factor):
    def block_of(position):
        return (jnp.arange(drawn.shape[position]) // (drawn.shape[position] // blocks)).reshape((-1,) + (1,) * (drawn.ndim - 1 - position))

    one_side = jax.random.permutation(rng, blocks)[block_of(target)]
    second = (block_of(target) + blocks // 2) % blocks
    return jnp.where((block_of(source) == one_side) | (block_of(source) == second), factor * drawn, drawn)


def steps_of(key, extent, shards, least, high):
    loudness, own = 1.0, jax.random.fold_in(key, 6)
    for axis_at, blocks in shards:
        heights = jnp.exp(jax.random.uniform(jax.random.fold_in(own, axis_at), (blocks,), jnp.float32, least / len(shards), high / len(shards)))
        loudness = loudness * jnp.repeat(heights, extent[axis_at] // blocks).reshape([-1 if axis == axis_at else 1 for axis in range(len(extent))])
    return loudness


def bell_draw(own_key, shape, deviation, bound, cuts=(), held_as=jnp.bfloat16):
    gain = steps_of(own_key, shape, cuts, -0.22, 0.18) if cuts else 1.0
    values = jax.random.normal(own_key, shape, jnp.float32) * deviation * gain
    return jnp.minimum(jnp.maximum(values, -bound), bound).astype(held_as)


def gaussian_with(own_key, shape, spread, reach, cuts, heavy, held_as=jnp.bfloat16):
    drawn = spread * jax.random.normal(own_key, shape, jnp.float32)
    if cuts:
        drawn = drawn * steps_of(own_key, shape, cuts, -0.22, 0.18)
    return jnp.clip(raised(drawn, jax.random.fold_in(own_key, 3), *heavy), -reach, reach).astype(held_as)


def setup_inputs(seed: int = 0) -> dict:
    splits = jax.random.split(jax.random.key(seed), 11)
    queries = bell_draw(splits[0], (N_DP, ROWS, D), 1.0, 6.0, ((0, 32), (1, 8)))
    keys = bell_draw(splits[1], (N_DP, ROWS, D), 1.0, 6.0, ((0, 32), (1, 8)))
    values = bell_draw(splits[2], (N_DP, ROWS, D), 1.0, 6.0, ((0, 32), (1, 8)))
    gates = bell_draw(splits[3], (N_DP, ROWS, D), 1.0, 6.0, ((0, 32), (1, 8)))
    cotangent = gaussian_with(splits[4], (N_DP, ROWS, D), 1.0, 6.0, ((0, 32), (1, 8)), (1, 2, 8, 2.0))
    out_weight = bell_draw(splits[5], (D, D), D ** -0.5, 0.1875)
    position_bias = bell_draw(splits[6], (HEADS, NBUCK), 1.0, 4.0, (), jnp.float32)
    distance_bucket = draw_distance_bucket(jax.random.fold_in(splits[10], 71), 0)
    history_lengths = draw_history_lengths(jax.random.fold_in(splits[10], 71), 0)
    first_device = with_ends(jax.random.randint(splits[9], (N_DP,), 0, N_CTX), jax.random.fold_in(splits[9], 1), 0, N_CTX - 1).astype(jnp.int32)
    return {"queries": queries, "keys": keys, "values": values, "gates": gates, "cotangent": cotangent, "out_weight": out_weight, "position_bias": position_bias, "distance_bucket": distance_bucket, "history_lengths": history_lengths, "first_device": first_device}


epsilon = 1e-05

def block_place(lengths_row, logical_block, block_rows):
    slot_count = lengths_row.shape[0]
    blocks_per = ((lengths_row + block_rows - 1) // block_rows).astype(jnp.int32)
    block_ends = jnp.cumsum(blocks_per).astype(jnp.int32)
    owner = jnp.sum((block_ends <= logical_block).astype(jnp.int32))
    chosen = jnp.arange(slot_count, dtype=jnp.int32) == owner
    user_len = jnp.sum(jnp.where(chosen, lengths_row, 0))
    user_end = jnp.sum(jnp.where(chosen, block_ends, 0))
    user_blocks = jnp.sum(jnp.where(chosen, blocks_per, 0))
    return (logical_block - (user_end - user_blocks), user_len)

def make_mask(offset, inner_block, user_len, block_rows):
    row_index = jnp.arange(block_rows, dtype=jnp.int32)
    query_live = inner_block * block_rows + row_index < user_len
    key_live = ((inner_block - offset) * block_rows + row_index < user_len) & (offset <= inner_block)
    pair_mask = query_live[:, None] & key_live[None, :]
    if offset == 0:
        pair_mask = pair_mask & (row_index[None, :] <= row_index[:, None])
    return pair_mask

def rounded(values_in):
    return lax.optimization_barrier(values_in.astype(jnp.bfloat16)).astype(jnp.float32)

def block_grads(query_rows, key_blocks, value_blocks, gate_rows, grad_out, out_weight, bias_dist, inner_block, user_len):
    block_rows, model_width = query_rows.shape
    head_count = bias_dist.shape[0]
    head_dim = model_width // head_count
    score_scale = head_dim ** (-0.5)
    row_index = jnp.arange(block_rows, dtype=jnp.int32)
    query_heads = query_rows.astype(jnp.float32).reshape(block_rows, head_count, head_dim)
    mixed_out = jnp.zeros((block_rows, model_width), jnp.float32)
    saved = []
    for offset in range(MAXB):
        key_heads = key_blocks[offset].astype(jnp.float32).reshape(block_rows, head_count, head_dim)
        value_heads = value_blocks[offset].astype(jnp.float32).reshape(block_rows, head_count, head_dim)
        distance_index = jnp.clip(offset * block_rows + row_index[:, None] - row_index[None, :], 0, MAXB * block_rows - 1)
        pair_bias = bias_dist[:, distance_index]
        pair_mask = make_mask(offset, inner_block, user_len, block_rows)
        score = score_scale * jnp.einsum('rhe,che->hrc', query_heads, key_heads) + pair_bias
        weight = rounded(jnp.where(pair_mask[None], jax.nn.silu(score), 0.0))
        mixed_out = mixed_out + jnp.einsum('hrc,che->rhe', weight, value_heads).reshape(block_rows, model_width)
        saved.append((key_heads, value_heads, score, weight, pair_mask))
    centered = mixed_out - lax.optimization_barrier(jnp.mean(mixed_out, axis=1, keepdims=True))
    inverse = lax.rsqrt(lax.optimization_barrier(jnp.mean(centered * centered, axis=1, keepdims=True)) + epsilon)
    normed = centered * inverse
    live = (inner_block * block_rows + row_index < user_len)[:, None]
    gate_float = gate_rows.astype(jnp.float32)
    gated_rows = jnp.where(live, normed * gate_float, 0.0).astype(jnp.bfloat16)
    d_gated = jnp.dot(grad_out, out_weight.T, preferred_element_type=jnp.float32)
    d_gates = jnp.where(live, d_gated * normed, 0.0).astype(jnp.bfloat16)
    d_normed = jnp.where(live, d_gated * gate_float, 0.0)
    d_mixed = inverse * (d_normed - lax.optimization_barrier(jnp.mean(d_normed, axis=1, keepdims=True)) - normed * lax.optimization_barrier(jnp.mean(d_normed * normed, axis=1, keepdims=True)))
    d_mixed_heads = rounded(d_mixed).reshape(block_rows, head_count, head_dim)
    d_query = jnp.zeros((block_rows, head_count, head_dim), jnp.float32)
    parts = []
    for key_heads, value_heads, score, weight, pair_mask in saved:
        d_attn = jnp.einsum('rhe,che->hrc', d_mixed_heads, value_heads)
        sigmoid_score = jax.nn.sigmoid(score)
        d_score = rounded(jnp.where(pair_mask[None], d_attn * sigmoid_score * (1.0 + score * (1.0 - sigmoid_score)), 0.0))
        d_query = d_query + jnp.einsum('hrc,che->rhe', d_score, key_heads)
        d_key = score_scale * jnp.einsum('hrc,rhe->che', d_score, query_heads)
        d_value = jnp.einsum('hrc,rhe->che', weight, d_mixed_heads)
        parts.append(jnp.stack([d_key.reshape(block_rows, model_width), d_value.reshape(block_rows, model_width)]))
    d_queries = (score_scale * d_query).reshape(block_rows, model_width).astype(jnp.bfloat16)
    return (d_queries, d_gates, gated_rows, jnp.stack(parts))

def reference(queries, keys, values, gates, cotangent, out_weight, position_bias, distance_bucket, history_lengths, first_device):
    group_count, ctx_rows, model_width = queries.shape
    ctx_count = history_lengths.shape[1]
    block_rows = ctx_rows // ctx_count
    bias_dist = position_bias[:, distance_bucket]

    def one_group(group_args):
        query_all, key_all, value_all, gate_all, grad_all, lengths_row, first_index = group_args
        logical_order = (first_index + jnp.arange(ctx_count, dtype=jnp.int32)) % ctx_count
        physical_order = (jnp.arange(ctx_count, dtype=jnp.int32) - first_index) % ctx_count

        def to_logical(rows_in):
            return jnp.take(rows_in.reshape(ctx_count, block_rows, model_width), logical_order, axis=0)
        query_log, key_log, value_log = (to_logical(query_all), to_logical(key_all), to_logical(value_all))
        gate_log, grad_log = (to_logical(gate_all), to_logical(grad_all))

        def one_block(logical_block):
            inner_block, user_len = block_place(lengths_row, logical_block, block_rows)
            sources = [((logical_block - offset) % ctx_count).astype(jnp.int32) for offset in range(MAXB)]
            key_blocks = [lax.dynamic_index_in_dim(key_log, source, 0, keepdims=False) for source in sources]
            value_blocks = [lax.dynamic_index_in_dim(value_log, source, 0, keepdims=False) for source in sources]
            query_rows = lax.dynamic_index_in_dim(query_log, logical_block, 0, keepdims=False)
            gate_rows = lax.dynamic_index_in_dim(gate_log, logical_block, 0, keepdims=False)
            grad_out = lax.dynamic_index_in_dim(grad_log, logical_block, 0, keepdims=False)
            return block_grads(query_rows, key_blocks, value_blocks, gate_rows, grad_out, out_weight, bias_dist, inner_block, user_len)
        d_query, d_gate, gated_rows, parts = lax.map(one_block, jnp.arange(ctx_count, dtype=jnp.int32))
        summed = parts[:, 0]
        for offset in range(1, MAXB):
            summed = summed + jnp.roll(parts[:, offset], -offset, axis=0)

        def to_physical(rows_in):
            return jnp.take(rows_in, physical_order, axis=0).reshape(ctx_rows, model_width)
        return (to_physical(d_query), to_physical(summed[:, 0].astype(jnp.bfloat16)), to_physical(summed[:, 1].astype(jnp.bfloat16)), to_physical(d_gate), to_physical(gated_rows))
    d_queries, d_keys, d_values, d_gates, gated_all = lax.map(one_group, (queries, keys, values, gates, cotangent, history_lengths, first_device))
    d_out_weight = jnp.dot(gated_all.reshape(-1, model_width).T, cotangent.reshape(-1, model_width), preferred_element_type=jnp.float32)
    return (d_queries, d_keys, d_values, d_gates, d_out_weight)
```

```python
import functools

import jax
import jax.numpy as jnp
from jax import lax
from jax.experimental import pallas as pl
from jax.experimental.pallas import tpu as pltpu
from jax.sharding import PartitionSpec as P

MESH = pl.DeviceIdType.MESH
F32 = jnp.float32
BF16 = jnp.bfloat16
EPS = 1e-05
HEADS = 8
HD = 128
ROWS = 256
HALF = 128
NCH = 16
SCALE = HD ** (-0.5)
GRIDS = {32: (4, 4, 2), 8: (2, 2, 2), 4: (1, 2, 2), 2: (1, 1, 2), 1: (1, 1, 1)}

LF = 2
LG = 4
LH = 6
SD = LH + 8
SFD = SD + 2
SB = SFD + 2
SC = SB + 2
SE = SC + 2
AHEAD = 2


def dot_nn(a, b):
    return lax.dot_general(a, b, (((1,), (0,)), ((), ())), preferred_element_type=F32)


def dot_nt(a, b):
    return lax.dot_general(a, b, (((1,), (1,)), ((), ())), preferred_element_type=F32)


def dot_tn(a, b):
    return lax.dot_general(a, b, (((0,), (0,)), ((), ())), preferred_element_type=F32)


def kernel(
    grid,
    n_ctx,
    q_hbm,
    k_hbm,
    v_hbm,
    g_hbm,
    c_hbm,
    w_hbm,
    pb_ref,
    db_ref,
    hl_ref,
    fd_ref,
    dq_hbm,
    dk_hbm,
    dv_hbm,
    dg_hbm,
    dw_ref,
    q0,
    k0,
    v0,
    g0,
    c0,
    w0,
    idx,
    vtab,
    tb,
    qin,
    p1f,
    mx,
    pout,
    pin,
    asav,
    dsav,
    dgf,
    dnc,
    gt,
    dm0,
    dmin,
    r0f,
    r1f,
    rout,
    rin,
    dka,
    dva,
    oq,
    ok,
    ov,
    og,
    wbuf,
    cin,
    c1,
    ain,
    bin_,
    a2,
    b2,
    a3in,
    b3in,
    fbuf,
    fin,
    lsem,
    osem,
    qs,
    qr,
    ps,
    pr,
    ds_,
    dr,
    rs,
    rr,
    cs,
    cr,
    as_,
    ar,
    bs,
    br,
    a3s,
    a3r,
    b3s,
    b3r,
    fs,
    fr,
):
    nx, ny, nc = grid
    dp = lax.axis_index("dp")
    ctx = lax.axis_index("ctx")
    xi = lax.div(dp, ny * nc)
    yi = lax.rem(lax.div(dp, nc), ny)
    ci = lax.rem(dp, nc)
    left = (dp, lax.rem(ctx + n_ctx - 1, n_ctx))
    right = (dp, lax.rem(ctx + 1, n_ctx))

    def at_x(k):
        return lax.rem(xi + k, nx)

    def at_y(k):
        return lax.rem(yi + k, ny)

    def dev(x, y, c):
        return (x * (ny * nc) + y * nc + c, ctx)

    other = 1 - ci
    peers = [(dp, lax.rem(ctx + k, n_ctx)) for k in range(1, n_ctx)]
    peers += [dev(at_x(k), yi, ci) for k in range(1, nx)]
    peers += [dev(xi, at_y(k), ci) for k in range(1, ny)]
    if nc > 1:
        peers.append(dev(xi, yi, other))

    loads = [
        pltpu.make_async_copy(src.at[0] if lead else src, dst, lsem.at[i])
        for i, (src, dst, lead) in enumerate(
            (
                (q_hbm, q0, True),
                (k_hbm, k0, True),
                (v_hbm, v0, True),
                (c_hbm, c0, True),
                (w_hbm, w0, False),
                (g_hbm, g0, True),
            )
        )
    ]
    barrier = pltpu.get_barrier_semaphore()
    for peer in peers:
        pl.semaphore_signal(barrier, inc=1, device_id=peer, device_id_type=MESH)
    for load in loads:
        load.start()

    block = lax.rem(ctx - fd_ref[0] + n_ctx, n_ctx)
    end = jnp.int32(0)
    inner = jnp.int32(0)
    user_len = jnp.int32(0)
    user_blocks = jnp.int32(0)
    for i in range(8):
        length = hl_ref[0, i]
        count = lax.div(length + (ROWS - 1), ROWS)
        start = end
        end = end + count
        inside = (start <= block) & (block < end)
        inner = jnp.where(inside, block - start, inner)
        user_len = jnp.where(inside, length, user_len)
        user_blocks = jnp.where(inside, count, user_blocks)
    live_rows = user_len - inner * ROWS
    valid = [
        None,
        (inner + 1 < user_blocks).astype(jnp.int32).astype(F32),
        (inner + 2 < user_blocks).astype(jnp.int32).astype(F32),
    ]

    def remote(src, dst, ssem, rsem, device):
        return pltpu.make_async_remote_copy(
            src_ref=src,
            dst_ref=dst,
            send_sem=ssem,
            recv_sem=rsem,
            device_id=device,
            device_id_type=MESH,
        )

    def half_of(n):
        return n // HEADS if isinstance(n, int) else lax.div(n, HEADS)

    def head_of(n):
        return n % HEADS if isinstance(n, int) else lax.rem(n, HEADS)

    def rows_of(n):
        r = half_of(n)
        return pl.ds(r * HALF if isinstance(n, int) else pl.multiple_of(r * HALF, HALF), HALF)

    def cols_of(n):
        h = head_of(n)
        return pl.ds(h * HD if isinstance(n, int) else pl.multiple_of(h * HD, HD), HD)

    def q_own(n):
        return remote(q0.at[rows_of(n), cols_of(n)], qin.at[0, n], qs.at[0, n], qr.at[0, n], left)

    def q_fwd(n):
        return remote(qin.at[0, n], qin.at[1, n], qs.at[1, n], qr.at[1, n], left)

    def p_two(n):
        return remote(pout.at[1, n], pin.at[1, n], ps.at[1, n], pr.at[1, n], right)

    def p_one(n):
        return remote(pout.at[0, n], pin.at[0, n], ps.at[0, n], pr.at[0, n], right)

    def d_own(n):
        return remote(dm0.at[n], dmin.at[0, n], ds_.at[0, n], dr.at[0, n], left)

    def d_fwd(n):
        return remote(dmin.at[0, n], dmin.at[1, n], ds_.at[1, n], dr.at[1, n], left)

    def r_two(n):
        return remote(rout.at[1, n], rin.at[1, n], rs.at[1, n], rr.at[1, n], right)

    def r_one(n):
        return remote(rout.at[0, n], rin.at[0, n], rs.at[0, n], rr.at[0, n], right)

    def tables():
        for m in range(6):
            idx[m : m + 1, :] = db_ref[m * HD : (m + 1) * HD].astype(F32).reshape(1, HD)
        idx[6:8, :] = jnp.zeros((2, HD), F32)
        rowi = lax.broadcasted_iota(jnp.int32, (HD, HD), 0)
        coli = lax.broadcasted_iota(jnp.int32, (HD, HD), 1)
        turn = jnp.where(rowi + coli == HD, 1.0, 0.0) + jnp.where(
            (rowi == 0) & (coli == 0), 1.0, 0.0
        )
        turned = dot_nn(idx[...].astype(BF16), turn.astype(BF16))
        lane = lax.broadcasted_iota(jnp.int32, (1, HD), 1)
        bias = pb_ref[...] * 0.5
        hi = bias.astype(BF16)
        rest = bias - hi.astype(F32)
        mid = rest.astype(BF16)
        low = (rest - mid.astype(F32)).astype(BF16)
        for m in range(7):
            before = turned[max(m - 1, 0) : max(m - 1, 0) + 1, :]
            here = turned[m : m + 1, :]
            want = jnp.where(lane == 0, here, before)
            hot = jnp.where(
                rowi.astype(F32) == jnp.broadcast_to(want, (HD, HD)), 1.0, 0.0
            ).astype(BF16)
            vtab[:, m * HD : (m + 1) * HD] = (
                dot_nn(hi, hot) + dot_nn(mid, hot) + dot_nn(low, hot)
            )

        def one_head(h, carry):
            tb[h, 0] = jnp.zeros((HD, HD), F32)
            for m in range(6):
                line = vtab[pl.ds(h, 1), m * HD : (m + 2) * HD]
                wide = jnp.broadcast_to(line, (HD, 2 * HD))
                tb[h, m + 1] = pltpu.roll(wide, 0, 1, stride=1, stride_axis=0)[:, :HD]
            return carry

        lax.fori_loop(0, HEADS, one_head, 0)

    def forward(n):
        r, h = half_of(n), head_of(n)
        kh, vh = k0[:, cols_of(n)], v0[:, cols_of(n)]
        for o in (2, 1, 0):
            qc = q0[rows_of(n), cols_of(n)] if o == 0 else qin[o - 1, n]
            bias = jnp.concatenate([tb[h, 2 * o + r + 1], tb[h, 2 * o + r]], axis=1)
            x = dot_nt(qc, kh) * (0.5 * SCALE) + bias
            th = jnp.tanh(x)
            u = 1.0 + th
            a = x * u
            d = u + a * (1.0 - th)
            if o == 0:
                row = lax.broadcasted_iota(jnp.int32, (HALF, ROWS), 0) + r * HALF
                col = lax.broadcasted_iota(jnp.int32, (HALF, ROWS), 1)
                a = jnp.where(col <= row, a, 0.0)
                d = jnp.where(col <= row, d, 0.0)
            a = a.astype(BF16)
            asav[o, n] = a
            dsav[o, n] = d
            part = dot_nn(a, vh)
            if o == 2:
                pout[1, n] = (part * valid[2]).astype(BF16)
                p_two(n).start()
            elif o == 1:
                p1f[n] = part * valid[1]
            else:
                mx[n] = part

    def backward(n):
        h = head_of(n)
        kh, vh = k0[:, cols_of(n)], v0[:, cols_of(n)]
        dss, dms = [], []
        for o in (2, 1, 0):
            if o == 0:
                dmc = dm0[n]
            else:
                dmc = (dmin[o - 1, n].astype(F32) * valid[o]).astype(BF16)
            dsc = (dot_nt(dmc, vh) * dsav[o, n]).astype(BF16)
            part = dot_nn(dsc, kh)
            if o == 2:
                rout[1, n] = part.astype(BF16)
                r_two(n).start()
            elif o == 1:
                r1f[n] = part
            else:
                r0f[n] = part
            dss.append(dsc)
            dms.append(dmc)
        qs3 = jnp.concatenate([qin[1, n], qin[0, n], q0[rows_of(n), cols_of(n)]], axis=0)
        dka[h] += dot_tn(jnp.concatenate(dss, axis=0), qs3)
        as3 = jnp.concatenate([asav[2, n], asav[1, n], asav[0, n]], axis=0)
        dva[h] += dot_tn(as3, jnp.concatenate(dms, axis=0))

    def live_mask(r, width):
        row = lax.broadcasted_iota(jnp.int32, (HALF, width), 0) + r * HALF
        return row < live_rows

    def gate_of(r, h):
        return g0[r * HALF : (r + 1) * HALF, h * HD : (h + 1) * HD].astype(F32)

    def d_gated():
        for i in (3, 4, 5):
            loads[i].wait()
        for pair in range(4):
            got = dot_nt(c0[...], w0[pair * 256 : (pair + 1) * 256, :])
            for r in range(2):
                for j in range(2):
                    h = 2 * pair + j
                    dgf[r * HEADS + h] = got[
                        r * HALF : (r + 1) * HALF, j * HD : (j + 1) * HD
                    ]
        for r in range(2):
            mask = live_mask(r, HD)
            total = jnp.zeros((HALF, HD), F32)
            for h in range(HEADS):
                dn = jnp.where(mask, dgf[r * HEADS + h] * gate_of(r, h), 0.0)
                dnc[r * HEADS + h] = dn
                total = total + dn
            mean = jnp.sum(total, axis=1, keepdims=True) * (1.0 / (HEADS * HD))
            for h in range(HEADS):
                dnc[r * HEADS + h] = dnc[r * HEADS + h] - mean

    def norm(r):
        inv_n = 1.0 / (HEADS * HD)
        total = mx[r * HEADS]
        for h in range(1, HEADS):
            total = total + mx[r * HEADS + h]
        mean = jnp.sum(total, axis=1, keepdims=True) * inv_n
        square = jnp.zeros((HALF, HD), F32)
        cross = jnp.zeros((HALF, HD), F32)
        for h in range(HEADS):
            cen = mx[r * HEADS + h] - mean
            mx[r * HEADS + h] = cen
            square = square + cen * cen
            cross = cross + cen * dnc[r * HEADS + h]
        inv = lax.rsqrt(jnp.sum(square, axis=1, keepdims=True) * inv_n + EPS)
        slope = jnp.sum(cross, axis=1, keepdims=True) * inv_n * inv * inv
        for h in range(HEADS):
            n = r * HEADS + h
            dm0[n] = (inv * (dnc[n] - mx[n] * slope)).astype(BF16)

        mask = live_mask(r, HD)
        rows = slice(r * HALF, (r + 1) * HALF)
        for h in range(HEADS):
            n = r * HEADS + h
            cols = slice(h * HD, (h + 1) * HD)
            normed = mx[n] * inv
            gt[rows, cols] = jnp.where(mask, normed * gate_of(r, h), 0.0).astype(BF16)
            og[rows, cols] = jnp.where(mask, dgf[n] * normed, 0.0).astype(BF16)

    rw = 1024 // (nx * ny * nc)

    def core_copy(x):
        return remote(wbuf.at[other, x], cin.at[x], cs.at[x], cr.at[x], dev(xi, yi, other))

    def a_copy(k):
        return remote(
            c1.at[at_x(k), :, 0], ain.at[k - 1], as_.at[k - 1], ar.at[k - 1], dev(at_x(k), yi, ci)
        )

    def b_copy(k):
        return remote(
            c1.at[:, at_y(k), 1], bin_.at[k - 1], bs.at[k - 1], br.at[k - 1], dev(xi, at_y(k), ci)
        )

    def a3_copy(k):
        return remote(
            a2.at[at_y(k)], a3in.at[k - 1], a3s.at[k - 1], a3r.at[k - 1], dev(xi, at_y(k), ci)
        )

    def b3_copy(k):
        return remote(
            b2.at[at_x(k)], b3in.at[k - 1], b3s.at[k - 1], b3r.at[k - 1], dev(at_x(k), yi, ci)
        )

    def f_copy(k):
        to = lax.rem(ctx + k, n_ctx)
        return remote(fbuf.at[to], fin.at[k - 1], fs.at[k - 1], fr.at[k - 1], (dp, to))

    def weight_terms():
        rx = 1024 // nx
        for x in range(nx):
            for half in range(2):
                got = dot_tn(
                    gt[:, x * rx : (x + 1) * rx], c0[:, half * 512 : (half + 1) * 512]
                ).astype(BF16)
                for y in range(ny):
                    for c in range(nc):
                        at = (y * nc + c) * rw
                        wbuf[c, x, y, half] = got[at : at + rw, :]
            if nc > 1:
                core_copy(x).start()

    def after_core():
        for x in range(nx):
            if nc > 1:
                core_copy(x).wait_recv()
            for y in range(ny):
                for half in range(2):
                    got = wbuf[ci, x, y, half].astype(F32)
                    if nc > 1:
                        got = got + cin[x, y, half].astype(F32)
                    c1[x, y, half] = got.astype(BF16)
        for k in range(1, nx):
            a_copy(k).start()
        for k in range(1, ny):
            b_copy(k).start()

    def after_two():
        for k in range(1, nx):
            a_copy(k).wait_recv()
        for y in range(ny):
            got = c1[xi, y, 0].astype(F32)
            for k in range(1, nx):
                got = got + ain[k - 1, y].astype(F32)
            a2[y] = got.astype(BF16)
        for k in range(1, ny):
            a3_copy(k).start()
        for k in range(1, ny):
            b_copy(k).wait_recv()
        for x in range(nx):
            got = c1[x, yi, 1].astype(F32)
            for k in range(1, ny):
                got = got + bin_[k - 1, x].astype(F32)
            b2[x] = got.astype(BF16)
        for k in range(1, nx):
            b3_copy(k).start()

    def after_three():
        for k in range(1, ny):
            a3_copy(k).wait_recv()
        got = a2[yi].astype(F32)
        for k in range(1, ny):
            got = got + a3in[k - 1].astype(F32)
        for c in range(4):
            fbuf[c] = got[:, c * HD : (c + 1) * HD].astype(BF16)
        for k in range(1, nx):
            b3_copy(k).wait_recv()
        got = b2[xi].astype(F32)
        for k in range(1, nx):
            got = got + b3in[k - 1].astype(F32)
        for c in range(4):
            fbuf[4 + c] = got[:, c * HD : (c + 1) * HD].astype(BF16)
        for k in range(1, n_ctx):
            f_copy(k).start()

    def after_four():
        for k in range(1, n_ctx):
            f_copy(k).wait_recv()
        got = fbuf[ctx].astype(F32)
        for k in range(1, n_ctx):
            got = got + fin[k - 1].astype(F32)
        dw_ref[...] = got

    outs = [
        pltpu.make_async_copy(src, dst.at[0], osem.at[i])
        for i, (src, dst) in enumerate(
            ((oq, dq_hbm), (ok, dk_hbm), (ov, dv_hbm), (og, dg_hbm))
        )
    ]

    def keys_out():
        for h in range(HEADS):
            cols = slice(h * HD, (h + 1) * HD)
            ok[:, cols] = (dka[h] * (0.5 * SCALE)).astype(BF16)
            ov[:, cols] = dva[h].astype(BF16)
        outs[1].start()
        outs[2].start()

    def st_q_own(n):
        q_own(n).start()

    def st_q_fwd(n):
        q_own(n).wait_recv()
        q_fwd(n).start()

    def st_forward(n):
        q_fwd(n).wait_recv()
        forward(n)

    def st_g(n):
        p_two(n).wait_recv()
        pout[0, n] = (p1f[n] + pin[1, n].astype(F32)).astype(BF16)
        p_one(n).start()

    def st_h(n):
        p_one(n).wait_recv()
        mx[n] += pin[0, n].astype(F32)

    def st_d_own(n):
        d_own(n).start()

    def st_d_fwd(n):
        d_own(n).wait_recv()
        d_fwd(n).start()

    def st_backward(n):
        d_fwd(n).wait_recv()
        backward(n)

    def st_c(n):
        r_two(n).wait_recv()
        rout[0, n] = (r1f[n] + rin[1, n].astype(F32)).astype(BF16)
        r_one(n).start()

    def st_e(n):
        r_one(n).wait_recv()
        oq[rows_of(n), cols_of(n)] = (
            (r0f[n] + rin[0, n].astype(F32)) * (0.5 * SCALE)
        ).astype(BF16)

    stages = (
        (st_q_own, -AHEAD),
        (st_d_own, SD),
        (st_q_fwd, 0),
        (st_d_fwd, SFD),
        (st_g, LG),
        (st_c, SC),
        (st_forward, LF),
        (st_backward, SB),
        (st_h, LH),
        (st_e, SE),
    )
    after = {
        5: [d_gated],
        LH + 7: [functools.partial(norm, 0)],
        LH + 15: [functools.partial(norm, 1), weight_terms, outs[3].start],
        LH + 18: [after_core],
        LH + 23: [after_two],
        LH + 27: [after_three, keys_out],
        SE + 15: [after_four],
    }

    loads[0].wait()
    pl.semaphore_wait(barrier, len(peers))
    for n in range(AHEAD):
        q_own(n).start()
    tables()
    loads[1].wait()
    loads[2].wait()
    dka[...] = jnp.zeros_like(dka)
    dva[...] = jnp.zeros_like(dva)

    last = SE + NCH

    def active(s):
        return tuple(0 <= s - at < NCH for _, at in stages)

    s = 0
    while s < last:
        e = s + 1
        while e < last and active(e) == active(s) and (e - 1) not in after:
            e += 1
        todo = [stage for stage, on in zip(stages, active(s)) if on]

        def slot(i, carry, todo=todo):
            for fn, at in todo:
                fn(i - at)
            return carry

        if e - s == 1:
            slot(s, 0)
        else:
            lax.fori_loop(s, e, slot, 0)
        for fn in after.get(e - 1, ()):
            fn()
        s = e
    outs[0].start()

    def drain(n, carry):
        for copy in (q_own, q_fwd, p_two, p_one, d_own, d_fwd, r_two, r_one):
            copy(n).wait_send()
        return carry

    lax.fori_loop(0, NCH, drain, 0)
    if nc > 1:
        for x in range(nx):
            core_copy(x).wait_send()
    for k in range(1, nx):
        a_copy(k).wait_send()
        b3_copy(k).wait_send()
    for k in range(1, ny):
        b_copy(k).wait_send()
        a3_copy(k).wait_send()
    for k in range(1, n_ctx):
        f_copy(k).wait_send()
    for out in outs:
        out.wait()


def on_device(q, k, v, g, c, w, pb, db, hl, fd):
    n_dp = lax.axis_size("dp")
    n_ctx = lax.axis_size("ctx")
    nx, ny, nc = grid = GRIDS[n_dp]
    rw = 1024 // n_dp
    chunk = (NCH, HALF, HD)
    vm = pltpu.VMEM
    dma = pltpu.SemaphoreType.DMA
    big = jax.ShapeDtypeStruct((1, ROWS, HEADS * HD), BF16)
    anyspec = pl.BlockSpec(memory_space=pl.ANY)
    vmem = pl.BlockSpec(memory_space=pltpu.VMEM)
    smem = pl.BlockSpec(memory_space=pltpu.SMEM)
    wide = vm((ROWS, HEADS * HD), BF16)
    return pl.pallas_call(
        functools.partial(kernel, grid, n_ctx),
        out_shape=(big, big, big, big, jax.ShapeDtypeStruct((rw, HD), F32)),
        in_specs=[anyspec] * 6 + [vmem, vmem, smem, smem],
        out_specs=[anyspec] * 4 + [vmem],
        scratch_shapes=[
            wide,
            wide,
            wide,
            wide,
            wide,
            vm((1024, 1024), BF16),
            vm((8, HD), F32),
            vm((HEADS, 7 * HD), F32),
            vm((HEADS, 7, HD, HD), F32),
            vm((2,) + chunk, BF16),
            vm(chunk, F32),
            vm(chunk, F32),
            vm((2,) + chunk, BF16),
            vm((2,) + chunk, BF16),
            vm((3, NCH, HALF, ROWS), BF16),
            vm((3, NCH, HALF, ROWS), F32),
            vm(chunk, F32),
            vm(chunk, F32),
            wide,
            vm(chunk, BF16),
            vm((2,) + chunk, BF16),
            vm(chunk, F32),
            vm(chunk, F32),
            vm((2,) + chunk, BF16),
            vm((2,) + chunk, BF16),
            vm((HEADS, ROWS, HD), F32),
            vm((HEADS, ROWS, HD), F32),
            wide,
            wide,
            wide,
            wide,
            vm((nc, nx, ny, 2, rw, 512), BF16),
            vm((nx, ny, 2, rw, 512), BF16),
            vm((nx, ny, 2, rw, 512), BF16),
            vm((max(nx - 1, 1), ny, rw, 512), BF16),
            vm((max(ny - 1, 1), nx, rw, 512), BF16),
            vm((ny, rw, 512), BF16),
            vm((nx, rw, 512), BF16),
            vm((max(ny - 1, 1), rw, 512), BF16),
            vm((max(nx - 1, 1), rw, 512), BF16),
            vm((8, rw, HD), BF16),
            vm((7, rw, HD), BF16),
            dma((6,)),
            dma((4,)),
        ]
        + [dma((2, NCH))] * 8
        + [dma((4,))] * 10
        + [dma((8,))] * 2,
        compiler_params=pltpu.CompilerParams(
            collective_id=0, has_side_effects=True, vmem_limit_bytes=60 * 1024 * 1024
        ),
    )(q, k, v, g, c, w, pb, db, hl, fd)


def solution(mesh):
    rows = P("dp", "ctx", None)
    return jax.shard_map(
        on_device,
        mesh=mesh,
        in_specs=(rows,) * 5 + (P(), P(), P(), P("dp", None), P("dp")),
        out_specs=(rows,) * 4 + (P("dp", "ctx"),),
        check_vma=False,
    )
```

```python
import functools
import math

import jax
import jax.numpy as jnp
from jax import lax
from jax.experimental import pallas as pl
from jax.experimental.pallas import tpu as pltpu
from jax.sharding import PartitionSpec as P

MESH = pl.DeviceIdType.MESH
F32 = jnp.float32
BF16 = jnp.bfloat16
EPS = 1e-05
HEADS = 8
HD = 128
ROWS = 256
HALF = 128
NCH = 16
SCALE = HD ** (-0.5)
GRIDS = {32: (4, 4, 2), 8: (2, 2, 2), 4: (1, 2, 2), 2: (1, 1, 2), 1: (1, 1, 1)}

MID = 6
PER = 7

AHEAD = 4.0
HOP = 3.5
MIDLAG = 0.4
T_OWN = 0.2
T_GATED = 8.95
D_LAG = 1.0
T_CORE = 3.0
T_TWO = 8.0
T_THREE = 11.5
T_FOUR = 14.5
T_MID = 0.4
DM = 2 * PER


def dot_nn(a, b):
    return lax.dot_general(a, b, (((1,), (0,)), ((), ())), preferred_element_type=F32)


def dot_nt(a, b):
    return lax.dot_general(a, b, (((1,), (1,)), ((), ())), preferred_element_type=F32)


def dot_tn(a, b):
    return lax.dot_general(a, b, (((0,), (0,)), ((), ())), preferred_element_type=F32)


def kernel(
    grid,
    n_ctx,
    q_hbm,
    k_hbm,
    v_hbm,
    g_hbm,
    c_hbm,
    w_hbm,
    pb_ref,
    db_ref,
    hl_ref,
    fd_ref,
    dq_hbm,
    dk_hbm,
    dv_hbm,
    dg_hbm,
    dw_ref,
    q0,
    k0,
    v0,
    g0,
    c0,
    w0,
    idx,
    vtab,
    tb,
    qin,
    p1f,
    mx,
    pout,
    pin,
    asav,
    dsav,
    dgf,
    dnc,
    gt,
    dm0,
    dmin,
    r0f,
    r1f,
    rout,
    rin,
    dka,
    dva,
    kl,
    vl,
    dkl,
    dvl,
    sout,
    sin,
    oq,
    ok,
    ov,
    og,
    wbuf,
    cin,
    c1,
    ain,
    bin_,
    a2,
    b2,
    a3in,
    b3in,
    fbuf,
    fin,
    lsem,
    osem,
    qs,
    qr,
    ps,
    pr,
    ds_,
    dr,
    rs,
    rr,
    ks,
    kr,
    ss,
    sr,
    cs,
    cr,
    as_,
    ar,
    bs,
    br,
    a3s,
    a3r,
    b3s,
    b3r,
    fs,
    fr,
):
    nx, ny, nc = grid
    dp = lax.axis_index("dp")
    ctx = lax.axis_index("ctx")
    xi = lax.div(dp, ny * nc)
    yi = lax.rem(lax.div(dp, nc), ny)
    ci = lax.rem(dp, nc)
    left = (dp, lax.rem(ctx + n_ctx - 1, n_ctx))
    right = (dp, lax.rem(ctx + 1, n_ctx))

    def at_x(k):
        return lax.rem(xi + k, nx)

    def at_y(k):
        return lax.rem(yi + k, ny)

    def dev(x, y, c):
        return (x * (ny * nc) + y * nc + c, ctx)

    other = 1 - ci
    peers = [(dp, lax.rem(ctx + k, n_ctx)) for k in range(1, n_ctx)]
    peers += [dev(at_x(k), yi, ci) for k in range(1, nx)]
    peers += [dev(xi, at_y(k), ci) for k in range(1, ny)]
    if nc > 1:
        peers.append(dev(xi, yi, other))

    loads = [
        pltpu.make_async_copy(src.at[0] if lead else src, dst, lsem.at[i])
        for i, (src, dst, lead) in enumerate(
            (
                (q_hbm, q0, True),
                (k_hbm, k0, True),
                (v_hbm, v0, True),
                (c_hbm, c0, True),
                (w_hbm, w0, False),
                (g_hbm, g0, True),
            )
        )
    ]
    barrier = pltpu.get_barrier_semaphore()
    for peer in peers:
        pl.semaphore_signal(barrier, inc=1, device_id=peer, device_id_type=MESH)
    for load in loads:
        load.start()

    block = lax.rem(ctx - fd_ref[0] + n_ctx, n_ctx)
    end = jnp.int32(0)
    inner = jnp.int32(0)
    user_len = jnp.int32(0)
    user_blocks = jnp.int32(0)
    for i in range(8):
        length = hl_ref[0, i]
        count = lax.div(length + (ROWS - 1), ROWS)
        start = end
        end = end + count
        inside = (start <= block) & (block < end)
        inner = jnp.where(inside, block - start, inner)
        user_len = jnp.where(inside, length, user_len)
        user_blocks = jnp.where(inside, count, user_blocks)
    live_rows = user_len - inner * ROWS
    valid = [
        None,
        (inner + 1 < user_blocks).astype(jnp.int32).astype(F32),
        (inner + 2 < user_blocks).astype(jnp.int32).astype(F32),
    ]
    valid_mid = ((inner >= 1) & (inner + 1 < user_blocks)).astype(jnp.int32).astype(F32)

    def remote(src, dst, ssem, rsem, device):
        return pltpu.make_async_remote_copy(
            src_ref=src,
            dst_ref=dst,
            send_sem=ssem,
            recv_sem=rsem,
            device_id=device,
            device_id_type=MESH,
        )

    def half_of(n):
        return n // HEADS if isinstance(n, int) else lax.div(n, HEADS)

    def head_of(n):
        return n % HEADS if isinstance(n, int) else lax.rem(n, HEADS)

    def rows_of(n):
        r = half_of(n)
        return pl.ds(r * HALF if isinstance(n, int) else pl.multiple_of(r * HALF, HALF), HALF)

    def cols_of(n):
        h = head_of(n)
        return pl.ds(h * HD if isinstance(n, int) else pl.multiple_of(h * HD, HD), HD)

    def q_own(n):
        return remote(q0.at[rows_of(n), cols_of(n)], qin.at[0, n], qs.at[0, n], qr.at[0, n], left)

    def q_fwd(n):
        return remote(qin.at[0, n], qin.at[1, n], qs.at[1, n], qr.at[1, n], left)

    def p_two(n):
        return remote(pout.at[1, n], pin.at[1, n], ps.at[1, n], pr.at[1, n], right)

    def p_one(n):
        return remote(pout.at[0, n], pin.at[0, n], ps.at[0, n], pr.at[0, n], right)

    def d_own(n):
        return remote(dm0.at[n], dmin.at[0, n], ds_.at[0, n], dr.at[0, n], left)

    def d_fwd(n):
        return remote(dmin.at[0, n], dmin.at[1, n], ds_.at[1, n], dr.at[1, n], left)

    def r_two(n):
        return remote(rout.at[1, n], rin.at[1, n], rs.at[1, n], rr.at[1, n], right)

    def r_one(n):
        return remote(rout.at[0, n], rin.at[0, n], rs.at[0, n], rr.at[0, n], right)

    def kv_own(i):
        src, dst = ((k0, kl), (v0, vl))[i % 2]
        h = i // 2
        return remote(
            src.at[:, pl.ds((MID + h) * HD, HD)], dst.at[h], ks.at[i], kr.at[i], right
        )

    def kv_back(i):
        return remote(sout.at[i], sin.at[i], ss.at[i], sr.at[i], left)

    def tables():
        for m in range(6):
            idx[m : m + 1, :] = db_ref[m * HD : (m + 1) * HD].astype(F32).reshape(1, HD)
        idx[6:8, :] = jnp.zeros((2, HD), F32)
        rowi = lax.broadcasted_iota(jnp.int32, (HD, HD), 0)
        coli = lax.broadcasted_iota(jnp.int32, (HD, HD), 1)
        turn = jnp.where(rowi + coli == HD, 1.0, 0.0) + jnp.where(
            (rowi == 0) & (coli == 0), 1.0, 0.0
        )
        turned = dot_nn(idx[...].astype(BF16), turn.astype(BF16))
        lane = lax.broadcasted_iota(jnp.int32, (1, HD), 1)
        bias = pb_ref[...] * 0.5
        hi = bias.astype(BF16)
        rest = bias - hi.astype(F32)
        mid = rest.astype(BF16)
        low = (rest - mid.astype(F32)).astype(BF16)
        for m in range(7):
            before = turned[max(m - 1, 0) : max(m - 1, 0) + 1, :]
            here = turned[m : m + 1, :]
            want = jnp.where(lane == 0, here, before)
            hot = jnp.where(
                rowi.astype(F32) == jnp.broadcast_to(want, (HD, HD)), 1.0, 0.0
            ).astype(BF16)
            vtab[:, m * HD : (m + 1) * HD] = (
                dot_nn(hi, hot) + dot_nn(mid, hot) + dot_nn(low, hot)
            )

        def one_head(h, carry):
            tb[h, 0] = jnp.zeros((HD, HD), F32)
            for m in range(6):
                line = vtab[pl.ds(h, 1), m * HD : (m + 2) * HD]
                wide = jnp.broadcast_to(line, (HD, 2 * HD))
                tb[h, m + 1] = pltpu.roll(wide, 0, 1, stride=1, stride_axis=0)[:, :HD]
            return carry

        lax.fori_loop(0, HEADS, one_head, 0)

    def curve(qc, kh, h, r, o):
        bias = jnp.concatenate([tb[h, 2 * o + r + 1], tb[h, 2 * o + r]], axis=1)
        x = dot_nt(qc, kh) * (0.5 * SCALE) + bias
        th = jnp.tanh(x)
        u = 1.0 + th
        a = x * u
        return a, u + a * (1.0 - th)

    def forward_own(n):
        r, h = half_of(n), head_of(n)
        a, d = curve(q0[rows_of(n), cols_of(n)], k0[:, cols_of(n)], h, r, 0)
        row = lax.broadcasted_iota(jnp.int32, (HALF, ROWS), 0) + r * HALF
        col = lax.broadcasted_iota(jnp.int32, (HALF, ROWS), 1)
        a = jnp.where(col <= row, a, 0.0).astype(BF16)
        asav[0, n] = a
        dsav[0, n] = jnp.where(col <= row, d, 0.0)
        mx[n] = dot_nn(a, v0[:, cols_of(n)])

    def forward(n):
        r, h = half_of(n), head_of(n)
        kh, vh = k0[:, cols_of(n)], v0[:, cols_of(n)]
        for o in (2, 1):
            a, d = curve(qin[o - 1, n], kh, h, r, o)
            a = a.astype(BF16)
            asav[o, n] = a
            dsav[o, n] = d
            part = dot_nn(a, vh) * valid[o]
            if o == 2:
                pout[1, n] = part.astype(BF16)
                p_two(n).start()
            else:
                p1f[n] = part

    def forward_mid(n):
        r, h = half_of(n), head_of(n)
        total = None
        for o in (1, 2):
            kh = k0[:, cols_of(n)] if o == 1 else kl[h - MID]
            vh = v0[:, cols_of(n)] if o == 1 else vl[h - MID]
            a, d = curve(qin[0, n], kh, h, r, o)
            a = a.astype(BF16)
            asav[o, n] = a
            dsav[o, n] = d
            part = dot_nn(a, vh) * (valid[1] if o == 1 else valid_mid)
            total = part if total is None else total + part
        pout[0, n] = total.astype(BF16)
        p_one(n).start()

    def masked(x, flag):
        return (x.astype(F32) * flag).astype(BF16)

    def backward(n):
        h = head_of(n)
        kh, vh = k0[:, cols_of(n)], v0[:, cols_of(n)]
        dss, dms = [], []
        for o in (2, 1, 0):
            dmc = dm0[n] if o == 0 else masked(dmin[o - 1, n], valid[o])
            dsc = (dot_nt(dmc, vh) * dsav[o, n]).astype(BF16)
            part = dot_nn(dsc, kh)
            if o == 2:
                rout[1, n] = part.astype(BF16)
                r_two(n).start()
            elif o == 1:
                r1f[n] = part
            else:
                r0f[n] = part
            dss.append(dsc)
            dms.append(dmc)
        qs3 = jnp.concatenate([qin[1, n], qin[0, n], q0[rows_of(n), cols_of(n)]], axis=0)
        dka[h] += dot_tn(jnp.concatenate(dss, axis=0), qs3)
        as3 = jnp.concatenate([asav[2, n], asav[1, n], asav[0, n]], axis=0)
        dva[h] += dot_tn(as3, jnp.concatenate(dms, axis=0))

    def backward_mid(n):
        h = head_of(n)
        i = h - MID
        kh, vh = k0[:, cols_of(n)], v0[:, cols_of(n)]
        near, far = masked(dmin[0, n], valid[1]), masked(dmin[0, n], valid_mid)
        ds_far = (dot_nt(far, vl[i]) * dsav[2, n]).astype(BF16)
        ds_near = (dot_nt(near, vh) * dsav[1, n]).astype(BF16)
        rout[0, n] = (dot_nn(ds_near, kh) + dot_nn(ds_far, kl[i])).astype(BF16)
        r_one(n).start()
        ds_own = (dot_nt(dm0[n], vh) * dsav[0, n]).astype(BF16)
        r0f[n] = dot_nn(ds_own, kh)
        qn = qin[0, n]
        dka[h] += dot_tn(
            jnp.concatenate([ds_near, ds_own], axis=0),
            jnp.concatenate([qn, q0[rows_of(n), cols_of(n)]], axis=0),
        )
        dva[h] += dot_tn(
            jnp.concatenate([asav[1, n], asav[0, n]], axis=0),
            jnp.concatenate([near, dm0[n]], axis=0),
        )
        dkl[i] += dot_tn(ds_far, qn)
        dvl[i] += dot_tn(asav[2, n], far)

    def mid_out():
        for i in range(HEADS - MID):
            sout[2 * i] = (dkl[i] * (0.5 * SCALE)).astype(BF16)
            sout[2 * i + 1] = dvl[i].astype(BF16)
            kv_back(2 * i).start()
            kv_back(2 * i + 1).start()

    def live_mask(r, width):
        row = lax.broadcasted_iota(jnp.int32, (HALF, width), 0) + r * HALF
        return row < live_rows

    def gate_of(r, h):
        return g0[r * HALF : (r + 1) * HALF, h * HD : (h + 1) * HD].astype(F32)

    def d_gated():
        for i in (3, 4, 5):
            loads[i].wait()
        for pair in range(4):
            got = dot_nt(c0[...], w0[pair * 256 : (pair + 1) * 256, :])
            for r in range(2):
                for j in range(2):
                    h = 2 * pair + j
                    dgf[r * HEADS + h] = got[
                        r * HALF : (r + 1) * HALF, j * HD : (j + 1) * HD
                    ]
        for r in range(2):
            mask = live_mask(r, HD)
            total = jnp.zeros((HALF, HD), F32)
            for h in range(HEADS):
                dn = jnp.where(mask, dgf[r * HEADS + h] * gate_of(r, h), 0.0)
                dnc[r * HEADS + h] = dn
                total = total + dn
            mean = jnp.sum(total, axis=1, keepdims=True) * (1.0 / (HEADS * HD))
            for h in range(HEADS):
                dnc[r * HEADS + h] = dnc[r * HEADS + h] - mean

    def norm(r):
        inv_n = 1.0 / (HEADS * HD)
        total = mx[r * HEADS]
        for h in range(1, HEADS):
            total = total + mx[r * HEADS + h]
        mean = jnp.sum(total, axis=1, keepdims=True) * inv_n
        square = jnp.zeros((HALF, HD), F32)
        cross = jnp.zeros((HALF, HD), F32)
        for h in range(HEADS):
            cen = mx[r * HEADS + h] - mean
            mx[r * HEADS + h] = cen
            square = square + cen * cen
            cross = cross + cen * dnc[r * HEADS + h]
        inv = lax.rsqrt(jnp.sum(square, axis=1, keepdims=True) * inv_n + EPS)
        slope = jnp.sum(cross, axis=1, keepdims=True) * inv_n * inv * inv
        for h in range(HEADS):
            n = r * HEADS + h
            dm0[n] = (inv * (dnc[n] - mx[n] * slope)).astype(BF16)

        mask = live_mask(r, HD)
        rows = slice(r * HALF, (r + 1) * HALF)
        for h in range(HEADS):
            n = r * HEADS + h
            cols = slice(h * HD, (h + 1) * HD)
            normed = mx[n] * inv
            gt[rows, cols] = jnp.where(mask, normed * gate_of(r, h), 0.0).astype(BF16)
            og[rows, cols] = jnp.where(mask, dgf[n] * normed, 0.0).astype(BF16)

    rw = 1024 // (nx * ny * nc)

    def core_copy(x):
        return remote(wbuf.at[other, x], cin.at[x], cs.at[x], cr.at[x], dev(xi, yi, other))

    def a_copy(k):
        return remote(
            c1.at[at_x(k), :, 0], ain.at[k - 1], as_.at[k - 1], ar.at[k - 1], dev(at_x(k), yi, ci)
        )

    def b_copy(k):
        return remote(
            c1.at[:, at_y(k), 1], bin_.at[k - 1], bs.at[k - 1], br.at[k - 1], dev(xi, at_y(k), ci)
        )

    def a3_copy(k):
        return remote(
            a2.at[at_y(k)], a3in.at[k - 1], a3s.at[k - 1], a3r.at[k - 1], dev(xi, at_y(k), ci)
        )

    def b3_copy(k):
        return remote(
            b2.at[at_x(k)], b3in.at[k - 1], b3s.at[k - 1], b3r.at[k - 1], dev(at_x(k), yi, ci)
        )

    def f_copy(k):
        to = lax.rem(ctx + k, n_ctx)
        return remote(fbuf.at[to], fin.at[k - 1], fs.at[k - 1], fr.at[k - 1], (dp, to))

    def weight_terms():
        rx = 1024 // nx
        for x in range(nx):
            for half in range(2):
                got = dot_tn(
                    gt[:, x * rx : (x + 1) * rx], c0[:, half * 512 : (half + 1) * 512]
                ).astype(BF16)
                for y in range(ny):
                    for c in range(nc):
                        at = (y * nc + c) * rw
                        wbuf[c, x, y, half] = got[at : at + rw, :]
            if nc > 1:
                core_copy(x).start()

    def after_core():
        for x in range(nx):
            if nc > 1:
                core_copy(x).wait_recv()
            for y in range(ny):
                for half in range(2):
                    got = wbuf[ci, x, y, half].astype(F32)
                    if nc > 1:
                        got = got + cin[x, y, half].astype(F32)
                    c1[x, y, half] = got.astype(BF16)
        for k in range(1, nx):
            a_copy(k).start()
        for k in range(1, ny):
            b_copy(k).start()

    def after_two():
        for k in range(1, nx):
            a_copy(k).wait_recv()
        for y in range(ny):
            got = c1[xi, y, 0].astype(F32)
            for k in range(1, nx):
                got = got + ain[k - 1, y].astype(F32)
            a2[y] = got.astype(BF16)
        for k in range(1, ny):
            a3_copy(k).start()
        for k in range(1, ny):
            b_copy(k).wait_recv()
        for x in range(nx):
            got = c1[x, yi, 1].astype(F32)
            for k in range(1, ny):
                got = got + bin_[k - 1, x].astype(F32)
            b2[x] = got.astype(BF16)
        for k in range(1, nx):
            b3_copy(k).start()

    def after_three():
        for k in range(1, ny):
            a3_copy(k).wait_recv()
        got = a2[yi].astype(F32)
        for k in range(1, ny):
            got = got + a3in[k - 1].astype(F32)
        for c in range(4):
            fbuf[c] = got[:, c * HD : (c + 1) * HD].astype(BF16)
        for k in range(1, nx):
            b3_copy(k).wait_recv()
        got = b2[xi].astype(F32)
        for k in range(1, nx):
            got = got + b3in[k - 1].astype(F32)
        for c in range(4):
            fbuf[4 + c] = got[:, c * HD : (c + 1) * HD].astype(BF16)
        for k in range(1, n_ctx):
            f_copy(k).start()

    def after_four():
        for k in range(1, n_ctx):
            f_copy(k).wait_recv()
        got = fbuf[ctx].astype(F32)
        for k in range(1, n_ctx):
            got = got + fin[k - 1].astype(F32)
        dw_ref[...] = got

    outs = [
        pltpu.make_async_copy(src, dst.at[0], osem.at[i])
        for i, (src, dst) in enumerate(
            ((oq, dq_hbm), (ok, dk_hbm), (ov, dv_hbm), (og, dg_hbm))
        )
    ]

    def keys_out():
        for h in range(MID):
            cols = slice(h * HD, (h + 1) * HD)
            ok[:, cols] = (dka[h] * (0.5 * SCALE)).astype(BF16)
            ov[:, cols] = dva[h].astype(BF16)

    def mid_in():
        for h in range(MID, HEADS):
            cols = slice(h * HD, (h + 1) * HD)
            i = 2 * (h - MID)
            kv_back(i).wait_recv()
            ok[:, cols] = (dka[h] * (0.5 * SCALE) + sin[i].astype(F32)).astype(BF16)
            kv_back(i + 1).wait_recv()
            ov[:, cols] = (dva[h] + sin[i + 1].astype(F32)).astype(BF16)
        outs[1].start()
        outs[2].start()

    def st_q_own(n):
        q_own(n).start()

    def st_q_fwd(n):
        q_own(n).wait_recv()
        q_fwd(n).start()

    def st_forward(n):
        q_fwd(n).wait_recv()
        forward(n)

    def st_g(n):
        p_two(n).wait_recv()
        pout[0, n] = (p1f[n] + pin[1, n].astype(F32)).astype(BF16)
        p_one(n).start()

    def st_h(n):
        p_one(n).wait_recv()
        mx[n] += pin[0, n].astype(F32)

    def st_d_own(n):
        d_own(n).start()

    def st_d_fwd(n):
        d_own(n).wait_recv()
        d_fwd(n).start()

    def st_backward(n):
        d_fwd(n).wait_recv()
        backward(n)

    def st_c(n):
        r_two(n).wait_recv()
        rout[0, n] = (r1f[n] + rin[1, n].astype(F32)).astype(BF16)
        r_one(n).start()

    def st_e(n):
        r_one(n).wait_recv()
        oq[rows_of(n), cols_of(n)] = (
            (r0f[n] + rin[0, n].astype(F32)) * (0.5 * SCALE)
        ).astype(BF16)

    def st_forward_mid(n):
        q_own(n).wait_recv()
        if n < HEADS:
            kv_own(2 * (n - MID)).wait_recv()
            kv_own(2 * (n - MID) + 1).wait_recv()
        forward_mid(n)

    def st_backward_mid(n):
        d_own(n).wait_recv()
        backward_mid(n)

    def once(fn):
        return lambda _: fn()

    events = []

    def at(time, fn, n=None):
        events.append((time, fn, n))

    for i in range(2 * (HEADS - MID)):
        at(-AHEAD - 0.1, once(kv_own(i).start))
    at(-0.01, once(tables))
    at(T_GATED, once(d_gated))
    first = 0
    for r in range(2):
        base = r * PER
        for h in range(MID):
            n, t = r * HEADS + h, base + h
            at(t - AHEAD, st_q_own, n)
            at(t, st_q_fwd, n)
            at(t + T_OWN, forward_own, n)
            at(t + HOP, st_forward, n)
            at(t + 2 * HOP, st_g, n)
            at(t + 3 * HOP, st_h, n)
        for i in range(HEADS - MID):
            n, t = r * HEADS + MID + i, base + MID + 0.5 * i
            at(t - AHEAD, st_q_own, n)
            at(t + T_OWN, forward_own, n)
            at(t + MIDLAG, st_forward_mid, n)
            at(t + MIDLAG + HOP, st_h, n)
        last_h = max(time for time, fn, n in events if fn is st_h)
        at(last_h + 0.01, once(functools.partial(norm, r)))
        first = max(DM + r * PER, math.ceil(last_h + D_LAG), first + PER)
        shift = 0 if r == 0 else 1
        for h in range(MID):
            n, t = r * HEADS + h, first + shift + h
            at(max(t - AHEAD, last_h + 0.02), st_d_own, n)
            at(t, st_d_fwd, n)
            at(t + HOP, st_backward, n)
            at(t + 2 * HOP, st_c, n)
            at(t + 3 * HOP, st_e, n)
        for i in range(HEADS - MID):
            n = r * HEADS + MID + i
            t = first + (MID if r == 0 else 0) + 0.5 * i
            at(max(t - AHEAD, last_h + 0.02), st_d_own, n)
            at(t + MIDLAG, st_backward_mid, n)
            at(t + MIDLAG + HOP, st_e, n)
    end = first + PER
    at(last_h + 0.5, once(weight_terms))
    at(last_h + 0.6, once(outs[3].start))
    at(last_h + T_CORE, once(after_core))
    at(last_h + T_TWO, once(after_two))
    at(last_h + T_THREE, once(after_three))
    at(last_h + T_FOUR, once(after_four))
    at(end + T_MID, once(mid_out))
    at(end + HOP, once(keys_out))
    at(end + 2 * HOP + 0.5, once(mid_in))

    slots = {}
    for time, fn, n in sorted(events, key=lambda e: e[0]):
        slots.setdefault(math.floor(time), []).append((fn, n))
    order = sorted(slots)

    def steps_of(s):
        return [(fn, None if n is None else n - s) for fn, n in slots[s]]

    dka[...] = jnp.zeros_like(dka)
    dva[...] = jnp.zeros_like(dva)
    dkl[...] = jnp.zeros_like(dkl)
    dvl[...] = jnp.zeros_like(dvl)

    loads[0].wait()
    loads[1].wait()
    loads[2].wait()
    pl.semaphore_wait(barrier, len(peers))
    i = 0
    while i < len(order):
        s = order[i]
        steps = steps_of(s)
        j = i + 1
        while (
            j < len(order)
            and order[j] == s + (j - i)
            and steps_of(order[j]) == steps
            and all(n is not None for _, n in steps)
        ):
            j += 1

        def slot(at_slot, carry, steps=steps):
            for fn, n in steps:
                fn(None if n is None else at_slot + n)
            return carry

        if j - i == 1:
            slot(s, 0)
        else:
            lax.fori_loop(s, s + (j - i), slot, 0)
        i = j
    outs[0].start()

    def drain(n, carry):
        for copy in (q_own, p_one, d_own, r_one):
            copy(n).wait_send()
        return carry

    def drain_two(h, carry):
        for r in range(2):
            for copy in (q_fwd, p_two, d_fwd, r_two):
                copy(r * HEADS + h).wait_send()
        return carry

    lax.fori_loop(0, NCH, drain, 0)
    lax.fori_loop(0, MID, drain_two, 0)
    for i in range(2 * (HEADS - MID)):
        kv_own(i).wait_send()
        kv_back(i).wait_send()
    if nc > 1:
        for x in range(nx):
            core_copy(x).wait_send()
    for k in range(1, nx):
        a_copy(k).wait_send()
        b3_copy(k).wait_send()
    for k in range(1, ny):
        b_copy(k).wait_send()
        a3_copy(k).wait_send()
    for k in range(1, n_ctx):
        f_copy(k).wait_send()
    for out in outs:
        out.wait()


def settle(n, *refs):
    srcs, dsts = refs[:n], refs[n : 2 * n]
    bufs, isem, osem = refs[2 * n : 3 * n], refs[3 * n], refs[3 * n + 1]
    ins = [pltpu.make_async_copy(s, b, isem.at[i]) for i, (s, b) in enumerate(zip(srcs, bufs))]
    outs = [pltpu.make_async_copy(b, d, osem.at[i]) for i, (b, d) in enumerate(zip(bufs, dsts))]
    for copy in ins:
        copy.start()
    for copy, out in zip(ins, outs):
        copy.wait()
        out.start()
    for out in outs:
        out.wait()


def settled(arrays):
    n = len(arrays)
    anyspec = pl.BlockSpec(memory_space=pl.ANY)
    shapes = tuple(jax.ShapeDtypeStruct(a.shape, a.dtype) for a in arrays)
    return pl.pallas_call(
        functools.partial(settle, n),
        out_shape=shapes,
        in_specs=[anyspec] * n,
        out_specs=[anyspec] * n,
        scratch_shapes=[pltpu.VMEM(a.shape, a.dtype) for a in arrays]
        + [pltpu.SemaphoreType.DMA((n,))] * 2,
        compiler_params=pltpu.CompilerParams(vmem_limit_bytes=60 * 1024 * 1024),
    )(*arrays)


def on_device(q, k, v, g, c, w, pb, db, hl, fd):
    n_dp = lax.axis_size("dp")
    n_ctx = lax.axis_size("ctx")
    nx, ny, nc = grid = GRIDS[n_dp]
    rw = 1024 // n_dp
    chunk = (NCH, HALF, HD)
    mids = HEADS - MID
    vm = pltpu.VMEM
    dma = pltpu.SemaphoreType.DMA
    big = jax.ShapeDtypeStruct((1, ROWS, HEADS * HD), BF16)
    anyspec = pl.BlockSpec(memory_space=pl.ANY)
    vmem = pl.BlockSpec(memory_space=pltpu.VMEM)
    smem = pl.BlockSpec(memory_space=pltpu.SMEM)
    wide = vm((ROWS, HEADS * HD), BF16)
    grads = pl.pallas_call(
        functools.partial(kernel, grid, n_ctx),
        out_shape=(big, big, big, big, jax.ShapeDtypeStruct((rw, HD), F32)),
        in_specs=[anyspec] * 6 + [vmem, vmem, smem, smem],
        out_specs=[anyspec] * 4 + [vmem],
        scratch_shapes=[
            wide,
            wide,
            wide,
            wide,
            wide,
            vm((1024, 1024), BF16),
            vm((8, HD), F32),
            vm((HEADS, 7 * HD), F32),
            vm((HEADS, 7, HD, HD), F32),
            vm((2,) + chunk, BF16),
            vm(chunk, F32),
            vm(chunk, F32),
            vm((2,) + chunk, BF16),
            vm((2,) + chunk, BF16),
            vm((3, NCH, HALF, ROWS), BF16),
            vm((3, NCH, HALF, ROWS), F32),
            vm(chunk, F32),
            vm(chunk, F32),
            wide,
            vm(chunk, BF16),
            vm((2,) + chunk, BF16),
            vm(chunk, F32),
            vm(chunk, F32),
            vm((2,) + chunk, BF16),
            vm((2,) + chunk, BF16),
            vm((HEADS, ROWS, HD), F32),
            vm((HEADS, ROWS, HD), F32),
            vm((mids, ROWS, HD), BF16),
            vm((mids, ROWS, HD), BF16),
            vm((mids, ROWS, HD), F32),
            vm((mids, ROWS, HD), F32),
            vm((2 * mids, ROWS, HD), BF16),
            vm((2 * mids, ROWS, HD), BF16),
            wide,
            wide,
            wide,
            wide,
            vm((nc, nx, ny, 2, rw, 512), BF16),
            vm((nx, ny, 2, rw, 512), BF16),
            vm((nx, ny, 2, rw, 512), BF16),
            vm((max(nx - 1, 1), ny, rw, 512), BF16),
            vm((max(ny - 1, 1), nx, rw, 512), BF16),
            vm((ny, rw, 512), BF16),
            vm((nx, rw, 512), BF16),
            vm((max(ny - 1, 1), rw, 512), BF16),
            vm((max(nx - 1, 1), rw, 512), BF16),
            vm((8, rw, HD), BF16),
            vm((7, rw, HD), BF16),
            dma((6,)),
            dma((4,)),
        ]
        + [dma((2, NCH))] * 8
        + [dma((2 * mids,))] * 4
        + [dma((4,))] * 10
        + [dma((8,))] * 2,
        compiler_params=pltpu.CompilerParams(
            collective_id=0, has_side_effects=True, vmem_limit_bytes=60 * 1024 * 1024
        ),
    )(q, k, v, g, c, w, pb, db, hl, fd)
    return settled(grads)


def solution(mesh):
    rows = P("dp", "ctx", None)
    return jax.shard_map(
        on_device,
        mesh=mesh,
        in_specs=(rows,) * 5 + (P(), P(), P(), P("dp", None), P("dp")),
        out_specs=(rows,) * 4 + (P("dp", "ctx"),),
        check_vma=False,
    )
```

```python
import functools
import math

import jax
import jax.numpy as jnp
from jax import lax
from jax.experimental import pallas as pl
from jax.experimental.pallas import tpu as pltpu
from jax.sharding import PartitionSpec as P

MESH = pl.DeviceIdType.MESH
F32 = jnp.float32
BF16 = jnp.bfloat16
EPS = 1e-05
HEADS = 8
HD = 128
ROWS = 256
HALF = 128
NCH = 16
SCALE = HD ** (-0.5)
GRIDS = {32: (4, 4, 2), 8: (2, 2, 2), 4: (1, 2, 2), 2: (1, 1, 2), 1: (1, 1, 1)}

MID = 5
MIDS = HEADS - MID
PAIRED = MID - MIDS
PER = MID

AHEAD = 4.0
HOP = 3.2
T_OWN = 0.2
T_GATED = 8.95
D_LAG = 1.0
T_CORE = 3.0
T_TWO = 8.0
T_THREE = 11.5
T_FOUR = 14.5


def dot_nn(a, b):
    return lax.dot_general(a, b, (((1,), (0,)), ((), ())), preferred_element_type=F32)


def dot_nt(a, b):
    return lax.dot_general(a, b, (((1,), (1,)), ((), ())), preferred_element_type=F32)


def dot_tn(a, b):
    return lax.dot_general(a, b, (((0,), (0,)), ((), ())), preferred_element_type=F32)


def kernel(
    grid,
    n_ctx,
    q_hbm,
    k_hbm,
    v_hbm,
    g_hbm,
    c_hbm,
    w_hbm,
    pb_ref,
    db_ref,
    hl_ref,
    fd_ref,
    dq_hbm,
    dk_hbm,
    dv_hbm,
    dg_hbm,
    dw_ref,
    q0,
    k0,
    v0,
    g0,
    c0,
    w0,
    idx,
    vtab,
    tb,
    qin,
    p1f,
    mx,
    pout,
    pin,
    asav,
    dsav,
    dgf,
    dnc,
    gt,
    dm0,
    dmin,
    r0f,
    r1f,
    rout,
    rin,
    dka,
    dva,
    kl,
    vl,
    dkl,
    dvl,
    sout,
    sin,
    qmux,
    dmux,
    oq,
    ok,
    ov,
    og,
    wbuf,
    cin,
    c1,
    ain,
    bin_,
    a2,
    b2,
    a3in,
    b3in,
    fbuf,
    fin,
    lsem,
    osem,
    qs,
    qr,
    ps,
    pr,
    ds_,
    dr,
    rs,
    rr,
    ks,
    kr,
    ss,
    sr,
    cs,
    cr,
    as_,
    ar,
    bs,
    br,
    a3s,
    a3r,
    b3s,
    b3r,
    fs,
    fr,
):
    nx, ny, nc = grid
    dp = lax.axis_index("dp")
    ctx = lax.axis_index("ctx")
    xi = lax.div(dp, ny * nc)
    yi = lax.rem(lax.div(dp, nc), ny)
    ci = lax.rem(dp, nc)
    left = (dp, lax.rem(ctx + n_ctx - 1, n_ctx))
    right = (dp, lax.rem(ctx + 1, n_ctx))

    def at_x(k):
        return lax.rem(xi + k, nx)

    def at_y(k):
        return lax.rem(yi + k, ny)

    def dev(x, y, c):
        return (x * (ny * nc) + y * nc + c, ctx)

    other = 1 - ci
    peers = [(dp, lax.rem(ctx + k, n_ctx)) for k in range(1, n_ctx)]
    peers += [dev(at_x(k), yi, ci) for k in range(1, nx)]
    peers += [dev(xi, at_y(k), ci) for k in range(1, ny)]
    if nc > 1:
        peers.append(dev(xi, yi, other))

    loads = [
        pltpu.make_async_copy(src.at[0] if lead else src, dst, lsem.at[i])
        for i, (src, dst, lead) in enumerate(
            (
                (q_hbm, q0, True),
                (k_hbm, k0, True),
                (v_hbm, v0, True),
                (c_hbm, c0, True),
                (w_hbm, w0, False),
                (g_hbm, g0, True),
            )
        )
    ]
    barrier = pltpu.get_barrier_semaphore()
    for peer in peers:
        pl.semaphore_signal(barrier, inc=1, device_id=peer, device_id_type=MESH)
    for load in loads:
        load.start()

    block = lax.rem(ctx - fd_ref[0] + n_ctx, n_ctx)
    end = jnp.int32(0)
    inner = jnp.int32(0)
    user_len = jnp.int32(0)
    user_blocks = jnp.int32(0)
    for i in range(8):
        length = hl_ref[0, i]
        count = lax.div(length + (ROWS - 1), ROWS)
        start = end
        end = end + count
        inside = (start <= block) & (block < end)
        inner = jnp.where(inside, block - start, inner)
        user_len = jnp.where(inside, length, user_len)
        user_blocks = jnp.where(inside, count, user_blocks)
    live_rows = user_len - inner * ROWS
    valid = [
        None,
        (inner + 1 < user_blocks).astype(jnp.int32).astype(F32),
        (inner + 2 < user_blocks).astype(jnp.int32).astype(F32),
    ]
    second = (inner == 1).astype(jnp.int32).astype(F32)
    third = (inner == 2).astype(jnp.int32).astype(F32)
    not_third = 1.0 - third
    middle = ((inner == 1) & (user_blocks == 3)).astype(jnp.int32).astype(F32)

    def remote(src, dst, ssem, rsem, device):
        return pltpu.make_async_remote_copy(
            src_ref=src,
            dst_ref=dst,
            send_sem=ssem,
            recv_sem=rsem,
            device_id=device,
            device_id_type=MESH,
        )

    def half_of(n):
        return n // HEADS if isinstance(n, int) else lax.div(n, HEADS)

    def head_of(n):
        return n % HEADS if isinstance(n, int) else lax.rem(n, HEADS)

    def rows_of(n):
        r = half_of(n)
        return pl.ds(r * HALF if isinstance(n, int) else pl.multiple_of(r * HALF, HALF), HALF)

    def cols_of(n):
        h = head_of(n)
        return pl.ds(h * HD if isinstance(n, int) else pl.multiple_of(h * HD, HD), HD)

    def q_own(n):
        return remote(q0.at[rows_of(n), cols_of(n)], qin.at[0, n], qs.at[0, n], qr.at[0, n], left)

    def q_fwd(n):
        return remote(qin.at[0, n], qin.at[1, n], qs.at[1, n], qr.at[1, n], left)

    def mux_at(n):
        return half_of(n) * MIDS + head_of(n) - PAIRED

    def q_fwd_paired(n):
        return remote(qmux.at[mux_at(n)], qin.at[1, n], qs.at[1, n], qr.at[1, n], left)

    def d_fwd_paired(n):
        return remote(dmux.at[mux_at(n)], dmin.at[1, n], ds_.at[1, n], dr.at[1, n], left)

    def p_two(n):
        return remote(pout.at[1, n], pin.at[1, n], ps.at[1, n], pr.at[1, n], right)

    def p_one(n):
        return remote(pout.at[0, n], pin.at[0, n], ps.at[0, n], pr.at[0, n], right)

    def d_own(n):
        return remote(dm0.at[n], dmin.at[0, n], ds_.at[0, n], dr.at[0, n], left)

    def d_fwd(n):
        return remote(dmin.at[0, n], dmin.at[1, n], ds_.at[1, n], dr.at[1, n], left)

    def r_two(n):
        return remote(rout.at[1, n], rin.at[1, n], rs.at[1, n], rr.at[1, n], right)

    def r_one(n):
        return remote(rout.at[0, n], rin.at[0, n], rs.at[0, n], rr.at[0, n], right)

    def kv_own(i):
        src, dst = ((k0, kl), (v0, vl))[i % 2]
        h = i // 2
        return remote(
            src.at[:, pl.ds((MID + h) * HD, HD)], dst.at[h], ks.at[i], kr.at[i], right
        )

    def kv_back(i):
        return remote(sout.at[i], sin.at[i], ss.at[i], sr.at[i], left)

    def tables():
        for m in range(6):
            idx[m : m + 1, :] = db_ref[m * HD : (m + 1) * HD].astype(F32).reshape(1, HD)
        idx[6:8, :] = jnp.zeros((2, HD), F32)
        rowi = lax.broadcasted_iota(jnp.int32, (HD, HD), 0)
        coli = lax.broadcasted_iota(jnp.int32, (HD, HD), 1)
        turn = jnp.where(rowi + coli == HD, 1.0, 0.0) + jnp.where(
            (rowi == 0) & (coli == 0), 1.0, 0.0
        )
        turned = dot_nn(idx[...].astype(BF16), turn.astype(BF16))
        lane = lax.broadcasted_iota(jnp.int32, (1, HD), 1)
        bias = pb_ref[...] * 0.5
        hi = bias.astype(BF16)
        rest = bias - hi.astype(F32)
        mid = rest.astype(BF16)
        low = (rest - mid.astype(F32)).astype(BF16)
        for m in range(7):
            before = turned[max(m - 1, 0) : max(m - 1, 0) + 1, :]
            here = turned[m : m + 1, :]
            want = jnp.where(lane == 0, here, before)
            hot = jnp.where(
                rowi.astype(F32) == jnp.broadcast_to(want, (HD, HD)), 1.0, 0.0
            ).astype(BF16)
            vtab[:, m * HD : (m + 1) * HD] = (
                dot_nn(hi, hot) + dot_nn(mid, hot) + dot_nn(low, hot)
            )

        def one_head(h, carry):
            tb[h, 0] = jnp.zeros((HD, HD), F32)
            for m in range(6):
                line = vtab[pl.ds(h, 1), m * HD : (m + 2) * HD]
                wide = jnp.broadcast_to(line, (HD, 2 * HD))
                tb[h, m + 1] = pltpu.roll(wide, 0, 1, stride=1, stride_axis=0)[:, :HD]
            return carry

        lax.fori_loop(0, HEADS, one_head, 0)

    def curve(qc, kh, h, r, o):
        bias = jnp.concatenate([tb[h, 2 * o + r + 1], tb[h, 2 * o + r]], axis=1)
        x = dot_nt(qc, kh) * (0.5 * SCALE) + bias
        th = jnp.tanh(x)
        u = 1.0 + th
        a = x * u
        return a, u + a * (1.0 - th)

    def forward_own(n):
        r, h = half_of(n), head_of(n)
        a, d = curve(q0[rows_of(n), cols_of(n)], k0[:, cols_of(n)], h, r, 0)
        row = lax.broadcasted_iota(jnp.int32, (HALF, ROWS), 0) + r * HALF
        col = lax.broadcasted_iota(jnp.int32, (HALF, ROWS), 1)
        a = jnp.where(col <= row, a, 0.0).astype(BF16)
        asav[0, n] = a
        dsav[0, n] = jnp.where(col <= row, d, 0.0)
        mx[n] = dot_nn(a, v0[:, cols_of(n)])

    def attend(qc, kh, vh, h, r, o, slot, n):
        a, d = curve(qc, kh, h, r, o)
        a = a.astype(BF16)
        asav[slot, n] = a
        dsav[slot, n] = d
        return dot_nn(a, vh)

    def forward(n, paired=False):
        r, h = half_of(n), head_of(n)
        kh, vh = k0[:, cols_of(n)], v0[:, cols_of(n)]
        two = attend(qin[1, n], kh, vh, h, r, 2, 2, n) * valid[2]
        if paired:
            m, hm, i = n + MIDS, h + MIDS, h - PAIRED
            km, vm = k0[:, cols_of(m)], v0[:, cols_of(m)]
            kb, vb = kl[i], vl[i]
            after = attend(qin[1, n], km, vm, hm, r, 1, 1, m)
            after = after + attend(qin[1, n], kb, vb, hm, r, 2, 2, m)
            two = two + after * middle
        pout[1, n] = two.astype(BF16)
        p_two(n).start()
        p1f[n] = attend(qin[0, n], kh, vh, h, r, 1, 1, n) * valid[1]
        if paired:
            mx[m] += attend(q0[rows_of(m), cols_of(m)], kb, vb, hm, r, 1, 3, m) * second

    def masked(x, flag):
        return (x.astype(F32) * flag).astype(BF16)

    def pull(dmc, kh, vh, slot, n):
        dsc = (dot_nt(dmc, vh) * dsav[slot, n]).astype(BF16)
        return dsc, dot_nn(dsc, kh)

    def backward(n, paired=False):
        h = head_of(n)
        kh, vh = k0[:, cols_of(n)], v0[:, cols_of(n)]
        dm_two = masked(dmin[1, n], valid[2])
        ds_two, part = pull(dm_two, kh, vh, 2, n)
        if paired:
            m, hm, i = n + MIDS, h + MIDS, h - PAIRED
            km, vm = k0[:, cols_of(m)], v0[:, cols_of(m)]
            kb, vb = kl[i], vl[i]
            dm_mid = masked(dmin[1, n], middle)
            ds_near, near = pull(dm_mid, km, vm, 1, m)
            ds_far, far = pull(dm_mid, kb, vb, 2, m)
            part = part + near + far
        rout[1, n] = part.astype(BF16)
        r_two(n).start()
        dm_one = masked(dmin[0, n], valid[1])
        ds_one, r1f[n] = pull(dm_one, kh, vh, 1, n)
        ds_own, r0f[n] = pull(dm0[n], kh, vh, 0, n)
        q_own_rows = q0[rows_of(n), cols_of(n)]
        dka[h] += dot_tn(
            jnp.concatenate([ds_two, ds_one, ds_own], axis=0),
            jnp.concatenate([qin[1, n], qin[0, n], q_own_rows], axis=0),
        )
        dva[h] += dot_tn(
            jnp.concatenate([asav[2, n], asav[1, n], asav[0, n]], axis=0),
            jnp.concatenate([dm_two, dm_one, dm0[n]], axis=0),
        )
        if paired:
            qm, qa = q0[rows_of(m), cols_of(m)], qin[1, n]
            dm_back = masked(dm0[m], second)
            ds_back, back = pull(dm_back, kb, vb, 3, m)
            ds_self, own = pull(dm0[m], km, vm, 0, m)
            r0f[m] = own + back
            dka[hm] += dot_tn(
                jnp.concatenate([ds_near, ds_self], axis=0), jnp.concatenate([qa, qm], axis=0)
            )
            dva[hm] += dot_tn(
                jnp.concatenate([asav[1, m], asav[0, m]], axis=0),
                jnp.concatenate([dm_mid, dm0[m]], axis=0),
            )
            dkl[i] += dot_tn(
                jnp.concatenate([ds_far, ds_back], axis=0), jnp.concatenate([qa, qm], axis=0)
            )
            dvl[i] += dot_tn(
                jnp.concatenate([asav[2, m], asav[3, m]], axis=0),
                jnp.concatenate([dm_mid, dm_back], axis=0),
            )

    def mid_out():
        for i in range(MIDS):
            sout[2 * i] = (dkl[i] * (0.5 * SCALE)).astype(BF16)
            sout[2 * i + 1] = dvl[i].astype(BF16)
            kv_back(2 * i).start()
            kv_back(2 * i + 1).start()

    def live_mask(r, width):
        row = lax.broadcasted_iota(jnp.int32, (HALF, width), 0) + r * HALF
        return row < live_rows

    def gate_of(r, h):
        return g0[r * HALF : (r + 1) * HALF, h * HD : (h + 1) * HD].astype(F32)

    def d_gated():
        for i in (3, 4, 5):
            loads[i].wait()
        for pair in range(4):
            got = dot_nt(c0[...], w0[pair * 256 : (pair + 1) * 256, :])
            for r in range(2):
                for j in range(2):
                    h = 2 * pair + j
                    dgf[r * HEADS + h] = got[
                        r * HALF : (r + 1) * HALF, j * HD : (j + 1) * HD
                    ]
        for r in range(2):
            mask = live_mask(r, HD)
            total = jnp.zeros((HALF, HD), F32)
            for h in range(HEADS):
                dn = jnp.where(mask, dgf[r * HEADS + h] * gate_of(r, h), 0.0)
                dnc[r * HEADS + h] = dn
                total = total + dn
            mean = jnp.sum(total, axis=1, keepdims=True) * (1.0 / (HEADS * HD))
            for h in range(HEADS):
                dnc[r * HEADS + h] = dnc[r * HEADS + h] - mean

    def norm(r):
        inv_n = 1.0 / (HEADS * HD)
        total = mx[r * HEADS]
        for h in range(1, HEADS):
            total = total + mx[r * HEADS + h]
        mean = jnp.sum(total, axis=1, keepdims=True) * inv_n
        square = jnp.zeros((HALF, HD), F32)
        cross = jnp.zeros((HALF, HD), F32)
        for h in range(HEADS):
            cen = mx[r * HEADS + h] - mean
            mx[r * HEADS + h] = cen
            square = square + cen * cen
            cross = cross + cen * dnc[r * HEADS + h]
        inv = lax.rsqrt(jnp.sum(square, axis=1, keepdims=True) * inv_n + EPS)
        slope = jnp.sum(cross, axis=1, keepdims=True) * inv_n * inv * inv
        for h in range(HEADS):
            n = r * HEADS + h
            dm0[n] = (inv * (dnc[n] - mx[n] * slope)).astype(BF16)

        mask = live_mask(r, HD)
        rows = slice(r * HALF, (r + 1) * HALF)
        for h in range(HEADS):
            n = r * HEADS + h
            cols = slice(h * HD, (h + 1) * HD)
            normed = mx[n] * inv
            gt[rows, cols] = jnp.where(mask, normed * gate_of(r, h), 0.0).astype(BF16)
            og[rows, cols] = jnp.where(mask, dgf[n] * normed, 0.0).astype(BF16)

    rw = 1024 // (nx * ny * nc)

    def core_copy(x):
        return remote(wbuf.at[other, x], cin.at[x], cs.at[x], cr.at[x], dev(xi, yi, other))

    def a_copy(k):
        return remote(
            c1.at[at_x(k), :, 0], ain.at[k - 1], as_.at[k - 1], ar.at[k - 1], dev(at_x(k), yi, ci)
        )

    def b_copy(k):
        return remote(
            c1.at[:, at_y(k), 1], bin_.at[k - 1], bs.at[k - 1], br.at[k - 1], dev(xi, at_y(k), ci)
        )

    def a3_copy(k):
        return remote(
            a2.at[at_y(k)], a3in.at[k - 1], a3s.at[k - 1], a3r.at[k - 1], dev(xi, at_y(k), ci)
        )

    def b3_copy(k):
        return remote(
            b2.at[at_x(k)], b3in.at[k - 1], b3s.at[k - 1], b3r.at[k - 1], dev(at_x(k), yi, ci)
        )

    def f_copy(k):
        to = lax.rem(ctx + k, n_ctx)
        return remote(fbuf.at[to], fin.at[k - 1], fs.at[k - 1], fr.at[k - 1], (dp, to))

    def weight_terms():
        rx = 1024 // nx
        for x in range(nx):
            for half in range(2):
                got = dot_tn(
                    gt[:, x * rx : (x + 1) * rx], c0[:, half * 512 : (half + 1) * 512]
                ).astype(BF16)
                for y in range(ny):
                    for c in range(nc):
                        at = (y * nc + c) * rw
                        wbuf[c, x, y, half] = got[at : at + rw, :]
            if nc > 1:
                core_copy(x).start()

    def after_core():
        for x in range(nx):
            if nc > 1:
                core_copy(x).wait_recv()
            for y in range(ny):
                for half in range(2):
                    got = wbuf[ci, x, y, half].astype(F32)
                    if nc > 1:
                        got = got + cin[x, y, half].astype(F32)
                    c1[x, y, half] = got.astype(BF16)
        for k in range(1, nx):
            a_copy(k).start()
        for k in range(1, ny):
            b_copy(k).start()

    def after_two():
        for k in range(1, nx):
            a_copy(k).wait_recv()
        for y in range(ny):
            got = c1[xi, y, 0].astype(F32)
            for k in range(1, nx):
                got = got + ain[k - 1, y].astype(F32)
            a2[y] = got.astype(BF16)
        for k in range(1, ny):
            a3_copy(k).start()
        for k in range(1, ny):
            b_copy(k).wait_recv()
        for x in range(nx):
            got = c1[x, yi, 1].astype(F32)
            for k in range(1, ny):
                got = got + bin_[k - 1, x].astype(F32)
            b2[x] = got.astype(BF16)
        for k in range(1, nx):
            b3_copy(k).start()

    def after_three():
        for k in range(1, ny):
            a3_copy(k).wait_recv()
        got = a2[yi].astype(F32)
        for k in range(1, ny):
            got = got + a3in[k - 1].astype(F32)
        for c in range(4):
            fbuf[c] = got[:, c * HD : (c + 1) * HD].astype(BF16)
        for k in range(1, nx):
            b3_copy(k).wait_recv()
        got = b2[xi].astype(F32)
        for k in range(1, nx):
            got = got + b3in[k - 1].astype(F32)
        for c in range(4):
            fbuf[4 + c] = got[:, c * HD : (c + 1) * HD].astype(BF16)
        for k in range(1, n_ctx):
            f_copy(k).start()

    def after_four():
        for k in range(1, n_ctx):
            f_copy(k).wait_recv()
        got = fbuf[ctx].astype(F32)
        for k in range(1, n_ctx):
            got = got + fin[k - 1].astype(F32)
        dw_ref[...] = got

    outs = [
        pltpu.make_async_copy(src, dst.at[0], osem.at[i])
        for i, (src, dst) in enumerate(
            ((oq, dq_hbm), (ok, dk_hbm), (ov, dv_hbm), (og, dg_hbm))
        )
    ]

    def keys_out():
        for h in range(MID):
            cols = slice(h * HD, (h + 1) * HD)
            ok[:, cols] = (dka[h] * (0.5 * SCALE)).astype(BF16)
            ov[:, cols] = dva[h].astype(BF16)

    def mid_in():
        for h in range(MID, HEADS):
            cols = slice(h * HD, (h + 1) * HD)
            i = 2 * (h - MID)
            kv_back(i).wait_recv()
            ok[:, cols] = (dka[h] * (0.5 * SCALE) + sin[i].astype(F32)).astype(BF16)
            kv_back(i + 1).wait_recv()
            ov[:, cols] = (dva[h] + sin[i + 1].astype(F32)).astype(BF16)
        outs[1].start()
        outs[2].start()

    def st_q_own(n):
        q_own(n).start()

    def st_q_fwd(n):
        q_own(n).wait_recv()
        q_fwd(n).start()

    def st_forward(n):
        q_fwd(n).wait_recv()
        forward(n)

    def st_g(n):
        p_two(n).wait_recv()
        pout[0, n] = (p1f[n] + pin[1, n].astype(F32)).astype(BF16)
        p_one(n).start()

    def st_h(n):
        p_one(n).wait_recv()
        mx[n] += pin[0, n].astype(F32)

    def st_d_own(n):
        d_own(n).start()

    def st_d_fwd(n):
        d_own(n).wait_recv()
        d_fwd(n).start()

    def st_backward(n):
        d_fwd(n).wait_recv()
        backward(n)

    def st_c(n):
        r_two(n).wait_recv()
        rout[0, n] = (r1f[n] + rin[1, n].astype(F32)).astype(BF16)
        r_one(n).start()

    def st_e(n):
        r_one(n).wait_recv()
        oq[rows_of(n), cols_of(n)] = (
            (r0f[n] + rin[0, n].astype(F32)) * (0.5 * SCALE)
        ).astype(BF16)

    def either(mine, passing):
        return (mine.astype(F32) * third + passing.astype(F32) * not_third).astype(BF16)

    def st_q_fwd_paired(n):
        m = n + MIDS
        q_own(n).wait_recv()
        qmux[mux_at(n)] = either(q0[rows_of(m), cols_of(m)], qin[0, n])
        q_fwd_paired(n).start()

    def st_d_fwd_paired(n):
        d_own(n).wait_recv()
        dmux[mux_at(n)] = either(dm0[n + MIDS], dmin[0, n])
        d_fwd_paired(n).start()

    def st_forward_paired(n):
        q_fwd(n).wait_recv()
        forward(n, True)

    def st_backward_paired(n):
        d_fwd(n).wait_recv()
        backward(n, True)

    def st_g_paired(n):
        p_two(n).wait_recv()
        got = pin[1, n].astype(F32)
        pout[0, n] = (p1f[n] + got * second).astype(BF16)
        p_one(n).start()
        mx[n + MIDS] += got * third

    def st_c_paired(n):
        r_two(n).wait_recv()
        got = rin[1, n].astype(F32)
        rout[0, n] = (r1f[n] + got * second).astype(BF16)
        r_one(n).start()
        m = n + MIDS
        oq[rows_of(m), cols_of(m)] = ((r0f[m] + got * third) * (0.5 * SCALE)).astype(BF16)

    def kv_wait(i):
        kv_own(2 * i).wait_recv()
        kv_own(2 * i + 1).wait_recv()

    def once(fn):
        return lambda _: fn()

    events = []

    def at(time, fn, n=None):
        events.append((time, fn, n))

    for i in range(2 * MIDS):
        at(-AHEAD - 0.1, once(kv_own(i).start))
    at(-0.01, once(tables))
    at(T_GATED, once(d_gated))
    first = 0
    for r in range(2):
        base = r * PER
        for h in range(MID):
            n, t, paired = r * HEADS + h, base + h, h >= PAIRED
            at(t - AHEAD, st_q_own, n)
            at(t, st_q_fwd_paired if paired else st_q_fwd, n)
            at(t + T_OWN, forward_own, n)
            if paired:
                at(t + T_OWN, forward_own, n + MIDS)
                if r == 0:
                    at(t + HOP - 0.01, once(functools.partial(kv_wait, h - PAIRED)))
            at(t + HOP, st_forward_paired if paired else st_forward, n)
            at(t + 2 * HOP, st_g_paired if paired else st_g, n)
            at(t + 3 * HOP, st_h, n)
        last_h = max(time for time, fn, n in events if fn is st_h)
        at(last_h + 0.01, once(functools.partial(norm, r)))
        first = max(2 * PER + r * PER, math.ceil(last_h + D_LAG), first + PER)
        for h in range(MID):
            n, t, paired = r * HEADS + h, first + h, h >= PAIRED
            at(max(t - AHEAD, last_h + 0.02), st_d_own, n)
            at(t, st_d_fwd_paired if paired else st_d_fwd, n)
            at(t + HOP, st_backward_paired if paired else st_backward, n)
            at(t + 2 * HOP, st_c_paired if paired else st_c, n)
            at(t + 3 * HOP, st_e, n)
    end = first + PER
    at(last_h + 0.5, once(weight_terms))
    at(last_h + 0.6, once(outs[3].start))
    at(last_h + T_CORE, once(after_core))
    at(last_h + T_TWO, once(after_two))
    at(last_h + T_THREE, once(after_three))
    at(last_h + T_FOUR, once(after_four))
    at(end - 1 + HOP + 0.02, once(mid_out))
    at(end - 1 + HOP + 0.03, once(keys_out))
    at(end - 1 + 3 * HOP + 0.1, once(mid_in))

    slots = {}
    for time, fn, n in sorted(events, key=lambda e: e[0]):
        slots.setdefault(math.floor(time), []).append((fn, n))
    order = sorted(slots)

    def steps_of(s):
        return [(fn, None if n is None else n - s) for fn, n in slots[s]]

    dka[...] = jnp.zeros_like(dka)
    dva[...] = jnp.zeros_like(dva)
    dkl[...] = jnp.zeros_like(dkl)
    dvl[...] = jnp.zeros_like(dvl)

    loads[0].wait()
    loads[1].wait()
    loads[2].wait()
    pl.semaphore_wait(barrier, len(peers))
    i = 0
    while i < len(order):
        s = order[i]
        steps = steps_of(s)
        j = i + 1
        while (
            j < len(order)
            and order[j] == s + (j - i)
            and steps_of(order[j]) == steps
            and all(n is not None for _, n in steps)
        ):
            j += 1

        def slot(at_slot, carry, steps=steps):
            for fn, n in steps:
                fn(None if n is None else at_slot + n)
            return carry

        if j - i == 1:
            slot(s, 0)
        else:
            lax.fori_loop(s, s + (j - i), slot, 0)
        i = j
    outs[0].start()

    def drain(h, carry):
        for r in range(2):
            n = r * HEADS + h
            for copy in (q_own, q_fwd, p_two, p_one, d_own, d_fwd, r_two, r_one):
                copy(n).wait_send()
        return carry

    lax.fori_loop(0, MID, drain, 0)
    for i in range(2 * MIDS):
        kv_own(i).wait_send()
        kv_back(i).wait_send()
    if nc > 1:
        for x in range(nx):
            core_copy(x).wait_send()
    for k in range(1, nx):
        a_copy(k).wait_send()
        b3_copy(k).wait_send()
    for k in range(1, ny):
        b_copy(k).wait_send()
        a3_copy(k).wait_send()
    for k in range(1, n_ctx):
        f_copy(k).wait_send()
    for out in outs:
        out.wait()


def settle(n, *refs):
    srcs, dsts = refs[:n], refs[n : 2 * n]
    bufs, isem, osem = refs[2 * n : 3 * n], refs[3 * n], refs[3 * n + 1]
    ins = [pltpu.make_async_copy(s, b, isem.at[i]) for i, (s, b) in enumerate(zip(srcs, bufs))]
    outs = [pltpu.make_async_copy(b, d, osem.at[i]) for i, (b, d) in enumerate(zip(bufs, dsts))]
    for copy in ins:
        copy.start()
    for copy, out in zip(ins, outs):
        copy.wait()
        out.start()
    for out in outs:
        out.wait()


def settled(arrays):
    n = len(arrays)
    anyspec = pl.BlockSpec(memory_space=pl.ANY)
    shapes = tuple(jax.ShapeDtypeStruct(a.shape, a.dtype) for a in arrays)
    return pl.pallas_call(
        functools.partial(settle, n),
        out_shape=shapes,
        in_specs=[anyspec] * n,
        out_specs=[anyspec] * n,
        scratch_shapes=[pltpu.VMEM(a.shape, a.dtype) for a in arrays]
        + [pltpu.SemaphoreType.DMA((n,))] * 2,
        compiler_params=pltpu.CompilerParams(vmem_limit_bytes=60 * 1024 * 1024),
    )(*arrays)


def on_device(q, k, v, g, c, w, pb, db, hl, fd):
    n_dp = lax.axis_size("dp")
    n_ctx = lax.axis_size("ctx")
    nx, ny, nc = grid = GRIDS[n_dp]
    rw = 1024 // n_dp
    chunk = (NCH, HALF, HD)
    vm = pltpu.VMEM
    dma = pltpu.SemaphoreType.DMA
    big = jax.ShapeDtypeStruct((1, ROWS, HEADS * HD), BF16)
    anyspec = pl.BlockSpec(memory_space=pl.ANY)
    vmem = pl.BlockSpec(memory_space=pltpu.VMEM)
    smem = pl.BlockSpec(memory_space=pltpu.SMEM)
    wide = vm((ROWS, HEADS * HD), BF16)
    grads = pl.pallas_call(
        functools.partial(kernel, grid, n_ctx),
        out_shape=(big, big, big, big, jax.ShapeDtypeStruct((rw, HD), F32)),
        in_specs=[anyspec] * 6 + [vmem, vmem, smem, smem],
        out_specs=[anyspec] * 4 + [vmem],
        scratch_shapes=[
            wide,
            wide,
            wide,
            wide,
            wide,
            vm((1024, 1024), BF16),
            vm((8, HD), F32),
            vm((HEADS, 7 * HD), F32),
            vm((HEADS, 7, HD, HD), F32),
            vm((2,) + chunk, BF16),
            vm(chunk, F32),
            vm(chunk, F32),
            vm((2,) + chunk, BF16),
            vm((2,) + chunk, BF16),
            vm((4, NCH, HALF, ROWS), BF16),
            vm((4, NCH, HALF, ROWS), F32),
            vm(chunk, F32),
            vm(chunk, F32),
            wide,
            vm(chunk, BF16),
            vm((2,) + chunk, BF16),
            vm(chunk, F32),
            vm(chunk, F32),
            vm((2,) + chunk, BF16),
            vm((2,) + chunk, BF16),
            vm((HEADS, ROWS, HD), F32),
            vm((HEADS, ROWS, HD), F32),
            vm((MIDS, ROWS, HD), BF16),
            vm((MIDS, ROWS, HD), BF16),
            vm((MIDS, ROWS, HD), F32),
            vm((MIDS, ROWS, HD), F32),
            vm((2 * MIDS, ROWS, HD), BF16),
            vm((2 * MIDS, ROWS, HD), BF16),
            vm((2 * MIDS, HALF, HD), BF16),
            vm((2 * MIDS, HALF, HD), BF16),
            wide,
            wide,
            wide,
            wide,
            vm((nc, nx, ny, 2, rw, 512), BF16),
            vm((nx, ny, 2, rw, 512), BF16),
            vm((nx, ny, 2, rw, 512), BF16),
            vm((max(nx - 1, 1), ny, rw, 512), BF16),
            vm((max(ny - 1, 1), nx, rw, 512), BF16),
            vm((ny, rw, 512), BF16),
            vm((nx, rw, 512), BF16),
            vm((max(ny - 1, 1), rw, 512), BF16),
            vm((max(nx - 1, 1), rw, 512), BF16),
            vm((8, rw, HD), BF16),
            vm((7, rw, HD), BF16),
            dma((6,)),
            dma((4,)),
        ]
        + [dma((2, NCH))] * 8
        + [dma((2 * MIDS,))] * 4
        + [dma((4,))] * 10
        + [dma((8,))] * 2,
        compiler_params=pltpu.CompilerParams(
            collective_id=0, has_side_effects=True, vmem_limit_bytes=60 * 1024 * 1024
        ),
    )(q, k, v, g, c, w, pb, db, hl, fd)
    return settled(grads)


def solution(mesh):
    rows = P("dp", "ctx", None)
    return jax.shard_map(
        on_device,
        mesh=mesh,
        in_specs=(rows,) * 5 + (P(), P(), P(), P("dp", None), P("dp")),
        out_specs=(rows,) * 4 + (P("dp", "ctx"),),
        check_vma=False,
    )
```

```python
import functools
import math

import jax
import jax.numpy as jnp
from jax import lax
from jax.experimental import pallas as pl
from jax.experimental.pallas import tpu as pltpu
from jax.sharding import PartitionSpec as P

MESH = pl.DeviceIdType.MESH
F32 = jnp.float32
BF16 = jnp.bfloat16
EPS = 1e-05
HEADS = 8
HD = 128
ROWS = 256
HALF = 128
NCH = 16
SCALE = HD ** (-0.5)
GRIDS = {32: (4, 4, 2), 8: (2, 2, 2), 4: (1, 2, 2), 2: (1, 1, 2), 1: (1, 1, 1)}

MID = 4
MIDS = HEADS - MID
PAIRED = MID - MIDS
PER = MID

AHEAD = 4.0
HOP = 3.2
T_OWN = 0.2
T_GATED = 8.95
D_LAG = 1.0
T_CORE = 3.0
T_TWO = 8.0
T_THREE = 11.5
T_FOUR = 14.5


def dot_nn(a, b):
    return lax.dot_general(a, b, (((1,), (0,)), ((), ())), preferred_element_type=F32)


def dot_nt(a, b):
    return lax.dot_general(a, b, (((1,), (1,)), ((), ())), preferred_element_type=F32)


def dot_tn(a, b):
    return lax.dot_general(a, b, (((0,), (0,)), ((), ())), preferred_element_type=F32)


def kernel(
    grid,
    n_ctx,
    q_hbm,
    k_hbm,
    v_hbm,
    g_hbm,
    c_hbm,
    w_hbm,
    pb_ref,
    db_ref,
    hl_ref,
    fd_ref,
    dq_hbm,
    dk_hbm,
    dv_hbm,
    dg_hbm,
    dw_ref,
    q0,
    k0,
    v0,
    g0,
    c0,
    w0,
    idx,
    vtab,
    tb,
    qin,
    p1f,
    mx,
    pout,
    pin,
    asav,
    dsav,
    dgf,
    dnc,
    gt,
    dm0,
    dmin,
    r0f,
    r1f,
    rout,
    rin,
    dka,
    dva,
    kl,
    vl,
    dkl,
    dvl,
    sout,
    sin,
    qmux,
    dmux,
    oq,
    ok,
    ov,
    og,
    wbuf,
    cin,
    c1,
    ain,
    bin_,
    a2,
    b2,
    a3in,
    b3in,
    fbuf,
    fin,
    lsem,
    osem,
    qs,
    qr,
    ps,
    pr,
    ds_,
    dr,
    rs,
    rr,
    ks,
    kr,
    ss,
    sr,
    cs,
    cr,
    as_,
    ar,
    bs,
    br,
    a3s,
    a3r,
    b3s,
    b3r,
    fs,
    fr,
    tell,
):
    nx, ny, nc = grid
    dp = lax.axis_index("dp")
    ctx = lax.axis_index("ctx")
    xi = lax.div(dp, ny * nc)
    yi = lax.rem(lax.div(dp, nc), ny)
    ci = lax.rem(dp, nc)
    left = (dp, lax.rem(ctx + n_ctx - 1, n_ctx))
    right = (dp, lax.rem(ctx + 1, n_ctx))

    def at_x(k):
        return lax.rem(xi + k, nx)

    def at_y(k):
        return lax.rem(yi + k, ny)

    def dev(x, y, c):
        return (x * (ny * nc) + y * nc + c, ctx)

    other = 1 - ci
    peers = [(dp, lax.rem(ctx + k, n_ctx)) for k in sorted({1, n_ctx - 1})]
    peers += [dev(at_x(k), yi, ci) for k in sorted({1, nx - 1} - {0})]
    peers += [dev(xi, at_y(k), ci) for k in sorted({1, ny - 1} - {0})]
    if nc > 1:
        peers.append(dev(xi, yi, other))

    loads = [
        pltpu.make_async_copy(src.at[0] if lead else src, dst, lsem.at[i])
        for i, (src, dst, lead) in enumerate(
            (
                (q_hbm, q0, True),
                (k_hbm, k0, True),
                (v_hbm, v0, True),
                (c_hbm, c0, True),
                (w_hbm, w0, False),
                (g_hbm, g0, True),
            )
        )
    ]
    barrier = pltpu.get_barrier_semaphore()
    for peer in peers:
        pl.semaphore_signal(barrier, inc=1, device_id=peer, device_id_type=MESH)
    for load in loads:
        load.start()

    block = lax.rem(ctx - fd_ref[0] + n_ctx, n_ctx)
    end = jnp.int32(0)
    inner = jnp.int32(0)
    user_len = jnp.int32(0)
    user_blocks = jnp.int32(0)
    for i in range(8):
        length = hl_ref[0, i]
        count = lax.div(length + (ROWS - 1), ROWS)
        start = end
        end = end + count
        inside = (start <= block) & (block < end)
        inner = jnp.where(inside, block - start, inner)
        user_len = jnp.where(inside, length, user_len)
        user_blocks = jnp.where(inside, count, user_blocks)
    live_rows = user_len - inner * ROWS
    valid = [
        None,
        (inner + 1 < user_blocks).astype(jnp.int32).astype(F32),
        (inner + 2 < user_blocks).astype(jnp.int32).astype(F32),
    ]
    second = (inner == 1).astype(jnp.int32).astype(F32)
    third = (inner == 2).astype(jnp.int32).astype(F32)
    not_third = 1.0 - third
    middle = ((inner == 1) & (user_blocks == 3)).astype(jnp.int32).astype(F32)

    def remote(src, dst, ssem, rsem, device):
        return pltpu.make_async_remote_copy(
            src_ref=src,
            dst_ref=dst,
            send_sem=ssem,
            recv_sem=rsem,
            device_id=device,
            device_id_type=MESH,
        )

    def half_of(n):
        return n // HEADS if isinstance(n, int) else lax.div(n, HEADS)

    def head_of(n):
        return n % HEADS if isinstance(n, int) else lax.rem(n, HEADS)

    def rows_of(n):
        r = half_of(n)
        return pl.ds(r * HALF if isinstance(n, int) else pl.multiple_of(r * HALF, HALF), HALF)

    def cols_of(n):
        h = head_of(n)
        return pl.ds(h * HD if isinstance(n, int) else pl.multiple_of(h * HD, HD), HD)

    def q_own(n):
        return remote(q0.at[rows_of(n), cols_of(n)], qin.at[0, n], qs.at[0, n], qr.at[0, n], left)

    def q_fwd(n):
        return remote(qin.at[0, n], qin.at[1, n], qs.at[1, n], qr.at[1, n], left)

    def mux_at(n):
        return half_of(n) * MIDS + head_of(n) - PAIRED

    def q_fwd_paired(n):
        return remote(qmux.at[mux_at(n)], qin.at[1, n], qs.at[1, n], qr.at[1, n], left)

    def d_fwd_paired(n):
        return remote(dmux.at[mux_at(n)], dmin.at[1, n], ds_.at[1, n], dr.at[1, n], left)

    def p_two(n):
        return remote(pout.at[1, n], pin.at[1, n], ps.at[1, n], pr.at[1, n], right)

    def p_one(n):
        return remote(pout.at[0, n], pin.at[0, n], ps.at[0, n], pr.at[0, n], right)

    def d_own(n):
        return remote(dm0.at[n], dmin.at[0, n], ds_.at[0, n], dr.at[0, n], left)

    def d_fwd(n):
        return remote(dmin.at[0, n], dmin.at[1, n], ds_.at[1, n], dr.at[1, n], left)

    def r_two(n):
        return remote(rout.at[1, n], rin.at[1, n], rs.at[1, n], rr.at[1, n], right)

    def r_one(n):
        return remote(rout.at[0, n], rin.at[0, n], rs.at[0, n], rr.at[0, n], right)

    def kv_own(i):
        src, dst = ((k0, kl), (v0, vl))[i % 2]
        h = i // 2
        return remote(
            src.at[:, pl.ds((MID + h) * HD, HD)], dst.at[h], ks.at[i], kr.at[i], right
        )

    def kv_back(i):
        return remote(sout.at[i], sin.at[i], ss.at[i], sr.at[i], left)

    def tables():
        for m in range(6):
            idx[m : m + 1, :] = db_ref[m * HD : (m + 1) * HD].astype(F32).reshape(1, HD)
        idx[6:8, :] = jnp.zeros((2, HD), F32)
        rowi = lax.broadcasted_iota(jnp.int32, (HD, HD), 0)
        coli = lax.broadcasted_iota(jnp.int32, (HD, HD), 1)
        turn = jnp.where(rowi + coli == HD, 1.0, 0.0) + jnp.where(
            (rowi == 0) & (coli == 0), 1.0, 0.0
        )
        turned = dot_nn(idx[...].astype(BF16), turn.astype(BF16))
        lane = lax.broadcasted_iota(jnp.int32, (1, HD), 1)
        bias = pb_ref[...] * 0.5
        hi = bias.astype(BF16)
        rest = bias - hi.astype(F32)
        mid = rest.astype(BF16)
        low = (rest - mid.astype(F32)).astype(BF16)
        for m in range(7):
            before = turned[max(m - 1, 0) : max(m - 1, 0) + 1, :]
            here = turned[m : m + 1, :]
            want = jnp.where(lane == 0, here, before)
            hot = jnp.where(
                rowi.astype(F32) == jnp.broadcast_to(want, (HD, HD)), 1.0, 0.0
            ).astype(BF16)
            vtab[:, m * HD : (m + 1) * HD] = (
                dot_nn(hi, hot) + dot_nn(mid, hot) + dot_nn(low, hot)
            )

        def one_head(h, carry):
            tb[h, 0] = jnp.zeros((HD, HD), F32)
            for m in range(6):
                line = vtab[pl.ds(h, 1), m * HD : (m + 2) * HD]
                wide = jnp.broadcast_to(line, (HD, 2 * HD))
                tb[h, m + 1] = pltpu.roll(wide, 0, 1, stride=1, stride_axis=0)[:, :HD]
            return carry

        lax.fori_loop(0, HEADS, one_head, 0)

    def curve(qc, kh, h, r, o):
        bias = jnp.concatenate([tb[h, 2 * o + r + 1], tb[h, 2 * o + r]], axis=1)
        x = dot_nt(qc, kh) * (0.5 * SCALE) + bias
        th = jnp.tanh(x)
        u = 1.0 + th
        a = x * u
        return a, u + a * (1.0 - th)

    def forward_own(n):
        r, h = half_of(n), head_of(n)
        a, d = curve(q0[rows_of(n), cols_of(n)], k0[:, cols_of(n)], h, r, 0)
        row = lax.broadcasted_iota(jnp.int32, (HALF, ROWS), 0) + r * HALF
        col = lax.broadcasted_iota(jnp.int32, (HALF, ROWS), 1)
        a = jnp.where(col <= row, a, 0.0).astype(BF16)
        asav[0, n] = a
        dsav[0, n] = jnp.where(col <= row, d, 0.0)
        mx[n] = dot_nn(a, v0[:, cols_of(n)])

    def attend(qc, kh, vh, h, r, o, slot, n):
        a, d = curve(qc, kh, h, r, o)
        a = a.astype(BF16)
        asav[slot, n] = a
        dsav[slot, n] = d
        return dot_nn(a, vh)

    def forward(n, paired=False):
        r, h = half_of(n), head_of(n)
        kh, vh = k0[:, cols_of(n)], v0[:, cols_of(n)]
        two = attend(qin[1, n], kh, vh, h, r, 2, 2, n) * valid[2]
        if paired:
            m, hm, i = n + MIDS, h + MIDS, h - PAIRED
            km, vm = k0[:, cols_of(m)], v0[:, cols_of(m)]
            kb, vb = kl[i], vl[i]
            after = attend(qin[1, n], km, vm, hm, r, 1, 1, m)
            after = after + attend(qin[1, n], kb, vb, hm, r, 2, 2, m)
            two = two + after * middle
        pout[1, n] = two.astype(BF16)
        p_two(n).start()
        p1f[n] = attend(qin[0, n], kh, vh, h, r, 1, 1, n) * valid[1]
        if paired:
            mx[m] += attend(q0[rows_of(m), cols_of(m)], kb, vb, hm, r, 1, 3, m) * second

    def masked(x, flag):
        return (x.astype(F32) * flag).astype(BF16)

    def pull(dmc, kh, vh, slot, n):
        dsc = (dot_nt(dmc, vh) * dsav[slot, n]).astype(BF16)
        return dsc, dot_nn(dsc, kh)

    def backward(n, paired=False):
        h = head_of(n)
        kh, vh = k0[:, cols_of(n)], v0[:, cols_of(n)]
        dm_two = masked(dmin[1, n], valid[2])
        ds_two, part = pull(dm_two, kh, vh, 2, n)
        if paired:
            m, hm, i = n + MIDS, h + MIDS, h - PAIRED
            km, vm = k0[:, cols_of(m)], v0[:, cols_of(m)]
            kb, vb = kl[i], vl[i]
            dm_mid = masked(dmin[1, n], middle)
            ds_near, near = pull(dm_mid, km, vm, 1, m)
            ds_far, far = pull(dm_mid, kb, vb, 2, m)
            part = part + near + far
        rout[1, n] = part.astype(BF16)
        r_two(n).start()
        dm_one = masked(dmin[0, n], valid[1])
        ds_one, r1f[n] = pull(dm_one, kh, vh, 1, n)
        ds_own, r0f[n] = pull(dm0[n], kh, vh, 0, n)
        q_own_rows = q0[rows_of(n), cols_of(n)]
        dka[h] += dot_tn(
            jnp.concatenate([ds_two, ds_one, ds_own], axis=0),
            jnp.concatenate([qin[1, n], qin[0, n], q_own_rows], axis=0),
        )
        dva[h] += dot_tn(
            jnp.concatenate([asav[2, n], asav[1, n], asav[0, n]], axis=0),
            jnp.concatenate([dm_two, dm_one, dm0[n]], axis=0),
        )
        if paired:
            qm, qa = q0[rows_of(m), cols_of(m)], qin[1, n]
            dm_back = masked(dm0[m], second)
            ds_back, back = pull(dm_back, kb, vb, 3, m)
            ds_self, own = pull(dm0[m], km, vm, 0, m)
            r0f[m] = own + back
            dka[hm] += dot_tn(
                jnp.concatenate([ds_near, ds_self], axis=0), jnp.concatenate([qa, qm], axis=0)
            )
            dva[hm] += dot_tn(
                jnp.concatenate([asav[1, m], asav[0, m]], axis=0),
                jnp.concatenate([dm_mid, dm0[m]], axis=0),
            )
            dkl[i] += dot_tn(
                jnp.concatenate([ds_far, ds_back], axis=0), jnp.concatenate([qa, qm], axis=0)
            )
            dvl[i] += dot_tn(
                jnp.concatenate([asav[2, m], asav[3, m]], axis=0),
                jnp.concatenate([dm_mid, dm_back], axis=0),
            )

    def mid_out(i):
        sout[2 * i] = (dkl[i] * (0.5 * SCALE)).astype(BF16)
        sout[2 * i + 1] = dvl[i].astype(BF16)
        kv_back(2 * i).start()
        kv_back(2 * i + 1).start()

    def live_mask(r, width):
        row = lax.broadcasted_iota(jnp.int32, (HALF, width), 0) + r * HALF
        return row < live_rows

    def gate_of(r, h):
        return g0[r * HALF : (r + 1) * HALF, h * HD : (h + 1) * HD].astype(F32)

    def d_gated():
        for i in (3, 4, 5):
            loads[i].wait()
        for pair in range(4):
            got = dot_nt(c0[...], w0[pair * 256 : (pair + 1) * 256, :])
            for r in range(2):
                for j in range(2):
                    h = 2 * pair + j
                    dgf[r * HEADS + h] = got[
                        r * HALF : (r + 1) * HALF, j * HD : (j + 1) * HD
                    ]
        for r in range(2):
            mask = live_mask(r, HD)
            total = jnp.zeros((HALF, HD), F32)
            for h in range(HEADS):
                dn = jnp.where(mask, dgf[r * HEADS + h] * gate_of(r, h), 0.0)
                dnc[r * HEADS + h] = dn
                total = total + dn
            mean = jnp.sum(total, axis=1, keepdims=True) * (1.0 / (HEADS * HD))
            for h in range(HEADS):
                dnc[r * HEADS + h] = dnc[r * HEADS + h] - mean

    def norm(r):
        inv_n = 1.0 / (HEADS * HD)
        total = mx[r * HEADS]
        for h in range(1, HEADS):
            total = total + mx[r * HEADS + h]
        mean = jnp.sum(total, axis=1, keepdims=True) * inv_n
        square = jnp.zeros((HALF, HD), F32)
        cross = jnp.zeros((HALF, HD), F32)
        for h in range(HEADS):
            cen = mx[r * HEADS + h] - mean
            mx[r * HEADS + h] = cen
            square = square + cen * cen
            cross = cross + cen * dnc[r * HEADS + h]
        inv = lax.rsqrt(jnp.sum(square, axis=1, keepdims=True) * inv_n + EPS)
        slope = jnp.sum(cross, axis=1, keepdims=True) * inv_n * inv * inv
        for h in range(HEADS):
            n = r * HEADS + h
            dm0[n] = (inv * (dnc[n] - mx[n] * slope)).astype(BF16)

        mask = live_mask(r, HD)
        rows = slice(r * HALF, (r + 1) * HALF)
        for h in range(HEADS):
            n = r * HEADS + h
            cols = slice(h * HD, (h + 1) * HD)
            normed = mx[n] * inv
            gt[rows, cols] = jnp.where(mask, normed * gate_of(r, h), 0.0).astype(BF16)
            og[rows, cols] = jnp.where(mask, dgf[n] * normed, 0.0).astype(BF16)

    rw = 1024 // (nx * ny * nc)

    def core_copy(x):
        return remote(wbuf.at[other, x], cin.at[x], cs.at[x], cr.at[x], dev(xi, yi, other))

    def a_copy(k):
        return remote(
            c1.at[at_x(k), :, 0], ain.at[k - 1], as_.at[k - 1], ar.at[k - 1], dev(at_x(k), yi, ci)
        )

    def b_copy(k):
        return remote(
            c1.at[:, at_y(k), 1], bin_.at[k - 1], bs.at[k - 1], br.at[k - 1], dev(xi, at_y(k), ci)
        )

    def a3_copy(k):
        return remote(
            a2.at[at_y(k)], a3in.at[k - 1], a3s.at[k - 1], a3r.at[k - 1], dev(xi, at_y(k), ci)
        )

    def b3_copy(k):
        return remote(
            b2.at[at_x(k)], b3in.at[k - 1], b3s.at[k - 1], b3r.at[k - 1], dev(at_x(k), yi, ci)
        )

    def f_copy(k):
        to = lax.rem(ctx + k, n_ctx)
        return remote(fbuf.at[to], fin.at[k - 1], fs.at[k - 1], fr.at[k - 1], (dp, to))

    def weight_terms():
        rx = 1024 // nx
        for x in range(nx):
            for half in range(2):
                got = dot_tn(
                    gt[:, x * rx : (x + 1) * rx], c0[:, half * 512 : (half + 1) * 512]
                ).astype(BF16)
                for y in range(ny):
                    for c in range(nc):
                        at = (y * nc + c) * rw
                        wbuf[c, x, y, half] = got[at : at + rw, :]
            if nc > 1:
                core_copy(x).start()

    def after_core():
        for x in range(nx):
            if nc > 1:
                core_copy(x).wait_recv()
            for y in range(ny):
                for half in range(2):
                    got = wbuf[ci, x, y, half].astype(F32)
                    if nc > 1:
                        got = got + cin[x, y, half].astype(F32)
                    c1[x, y, half] = got.astype(BF16)
        if nx == 4:
            pl.semaphore_wait(tell.at[0], 1)
        if ny == 4:
            pl.semaphore_wait(tell.at[1], 1)
        for k in range(1, nx):
            a_copy(k).start()
        for k in range(1, ny):
            b_copy(k).start()

    def after_two():
        for k in range(1, nx):
            a_copy(k).wait_recv()
        for y in range(ny):
            got = c1[xi, y, 0].astype(F32)
            for k in range(1, nx):
                got = got + ain[k - 1, y].astype(F32)
            a2[y] = got.astype(BF16)
        for k in range(1, ny):
            a3_copy(k).start()
        for k in range(1, ny):
            b_copy(k).wait_recv()
        for x in range(nx):
            got = c1[x, yi, 1].astype(F32)
            for k in range(1, ny):
                got = got + bin_[k - 1, x].astype(F32)
            b2[x] = got.astype(BF16)
        for k in range(1, nx):
            b3_copy(k).start()

    def after_three():
        for k in range(1, ny):
            a3_copy(k).wait_recv()
        got = a2[yi].astype(F32)
        for k in range(1, ny):
            got = got + a3in[k - 1].astype(F32)
        for c in range(4):
            fbuf[c] = got[:, c * HD : (c + 1) * HD].astype(BF16)
        for k in range(1, nx):
            b3_copy(k).wait_recv()
        got = b2[xi].astype(F32)
        for k in range(1, nx):
            got = got + b3in[k - 1].astype(F32)
        for c in range(4):
            fbuf[4 + c] = got[:, c * HD : (c + 1) * HD].astype(BF16)
        for k in range(1, n_ctx):
            f_copy(k).start()

    def after_four():
        for k in range(1, n_ctx):
            f_copy(k).wait_recv()
        got = fbuf[ctx].astype(F32)
        for k in range(1, n_ctx):
            got = got + fin[k - 1].astype(F32)
        dw_ref[...] = got

    outs = [
        pltpu.make_async_copy(src, dst.at[0], osem.at[i])
        for i, (src, dst) in enumerate(
            ((oq, dq_hbm), (ok, dk_hbm), (ov, dv_hbm), (og, dg_hbm))
        )
    ]

    def keys_out():
        for h in range(MID):
            cols = slice(h * HD, (h + 1) * HD)
            ok[:, cols] = (dka[h] * (0.5 * SCALE)).astype(BF16)
            ov[:, cols] = dva[h].astype(BF16)

    def mid_in():
        for h in range(MID, HEADS):
            cols = slice(h * HD, (h + 1) * HD)
            i = 2 * (h - MID)
            kv_back(i).wait_recv()
            ok[:, cols] = (dka[h] * (0.5 * SCALE) + sin[i].astype(F32)).astype(BF16)
            kv_back(i + 1).wait_recv()
            ov[:, cols] = (dva[h] + sin[i + 1].astype(F32)).astype(BF16)
        outs[1].start()
        outs[2].start()

    def st_q_own(n):
        q_own(n).start()

    def st_q_fwd(n):
        q_own(n).wait_recv()
        q_fwd(n).start()

    def st_forward(n):
        q_fwd(n).wait_recv()
        forward(n)

    def st_g(n):
        p_two(n).wait_recv()
        pout[0, n] = (p1f[n] + pin[1, n].astype(F32)).astype(BF16)
        p_one(n).start()

    def st_h(n):
        p_one(n).wait_recv()
        mx[n] += pin[0, n].astype(F32)

    def st_d_own(n):
        d_own(n).start()

    def st_d_fwd(n):
        d_own(n).wait_recv()
        d_fwd(n).start()

    def st_backward(n):
        d_fwd(n).wait_recv()
        backward(n)

    def st_c(n):
        r_two(n).wait_recv()
        rout[0, n] = (r1f[n] + rin[1, n].astype(F32)).astype(BF16)
        r_one(n).start()

    def st_e(n):
        r_one(n).wait_recv()
        oq[rows_of(n), cols_of(n)] = (
            (r0f[n] + rin[0, n].astype(F32)) * (0.5 * SCALE)
        ).astype(BF16)

    def either(mine, passing):
        return (mine.astype(F32) * third + passing.astype(F32) * not_third).astype(BF16)

    def st_q_fwd_paired(n):
        m = n + MIDS
        q_own(n).wait_recv()
        qmux[mux_at(n)] = either(q0[rows_of(m), cols_of(m)], qin[0, n])
        q_fwd_paired(n).start()

    def st_d_fwd_paired(n):
        d_own(n).wait_recv()
        dmux[mux_at(n)] = either(dm0[n + MIDS], dmin[0, n])
        d_fwd_paired(n).start()

    def st_forward_paired(n):
        q_fwd(n).wait_recv()
        forward(n, True)

    def st_backward_paired(n):
        d_fwd(n).wait_recv()
        backward(n, True)

    def st_g_paired(n):
        p_two(n).wait_recv()
        got = pin[1, n].astype(F32)
        pout[0, n] = (p1f[n] + got * second).astype(BF16)
        p_one(n).start()
        mx[n + MIDS] += got * third

    def st_c_paired(n):
        r_two(n).wait_recv()
        got = rin[1, n].astype(F32)
        rout[0, n] = (r1f[n] + got * second).astype(BF16)
        r_one(n).start()
        m = n + MIDS
        oq[rows_of(m), cols_of(m)] = ((r0f[m] + got * third) * (0.5 * SCALE)).astype(BF16)

    def kv_wait(i):
        kv_own(2 * i).wait_recv()
        kv_own(2 * i + 1).wait_recv()

    def once(fn):
        return lambda _: fn()

    events = []

    def at(time, fn, n=None):
        events.append((time, fn, n))

    for i in range(2 * MIDS):
        at(-AHEAD - 0.1, once(kv_own(i).start))
    at(-0.01, once(tables))
    at(T_GATED, once(d_gated))
    first = 0
    for r in range(2):
        base = r * PER
        for h in range(MID):
            n, t, paired = r * HEADS + h, base + h, h >= PAIRED
            at(t - AHEAD, st_q_own, n)
            at(t, st_q_fwd_paired if paired else st_q_fwd, n)
            at(t + T_OWN, forward_own, n)
            if paired:
                at(t + T_OWN, forward_own, n + MIDS)
                if r == 0:
                    at(t + HOP - 0.01, once(functools.partial(kv_wait, h - PAIRED)))
            at(t + HOP, st_forward_paired if paired else st_forward, n)
            at(t + 2 * HOP, st_g_paired if paired else st_g, n)
            at(t + 3 * HOP, st_h, n)
        last_h = max(time for time, fn, n in events if fn is st_h)
        at(last_h + 0.01, once(functools.partial(norm, r)))
        first = max(2 * PER + r * PER, math.ceil(last_h + D_LAG), first + PER)
        turn = list(range(MID))
        if r == 1:
            turn = turn[PAIRED:] + turn[:PAIRED]
        for place, h in enumerate(turn):
            n, t, paired = r * HEADS + h, first + place, h >= PAIRED
            if r == 1 and paired:
                at(t + HOP + 0.02, once(functools.partial(mid_out, h - PAIRED)))
            at(max(t - AHEAD, last_h + 0.02), st_d_own, n)
            at(t, st_d_fwd_paired if paired else st_d_fwd, n)
            at(t + HOP, st_backward_paired if paired else st_backward, n)
            at(t + 2 * HOP, st_c_paired if paired else st_c, n)
            at(t + 3 * HOP, st_e, n)
    end = first + PER
    at(last_h + 0.5, once(weight_terms))
    at(last_h + 0.6, once(outs[3].start))
    at(last_h + T_CORE, once(after_core))
    at(last_h + T_TWO, once(after_two))
    at(last_h + T_THREE, once(after_three))
    at(last_h + T_FOUR, once(after_four))
    at(end - 1 + HOP + 0.03, once(keys_out))
    at(end - 1 + 3 * HOP + 0.1, once(mid_in))

    slots = {}
    for time, fn, n in sorted(events, key=lambda e: e[0]):
        slots.setdefault(math.floor(time), []).append((fn, n))
    order = sorted(slots)

    def steps_of(s):
        return [(fn, None if n is None else n - s) for fn, n in slots[s]]

    dka[...] = jnp.zeros_like(dka)
    dva[...] = jnp.zeros_like(dva)
    dkl[...] = jnp.zeros_like(dkl)
    dvl[...] = jnp.zeros_like(dvl)

    loads[0].wait()
    loads[1].wait()
    loads[2].wait()
    pl.semaphore_wait(barrier, len(peers))
    if nx == 4:
        pl.semaphore_signal(tell.at[0], inc=1, device_id=dev(at_x(3), yi, ci), device_id_type=MESH)
    if ny == 4:
        pl.semaphore_signal(tell.at[1], inc=1, device_id=dev(xi, at_y(3), ci), device_id_type=MESH)
    i = 0
    while i < len(order):
        s = order[i]
        steps = steps_of(s)
        j = i + 1
        while (
            j < len(order)
            and order[j] == s + (j - i)
            and steps_of(order[j]) == steps
            and all(n is not None for _, n in steps)
        ):
            j += 1

        def slot(at_slot, carry, steps=steps):
            for fn, n in steps:
                fn(None if n is None else at_slot + n)
            return carry

        if j - i == 1:
            slot(s, 0)
        else:
            lax.fori_loop(s, s + (j - i), slot, 0)
        i = j
    outs[0].start()

    def drain(h, carry):
        for r in range(2):
            n = r * HEADS + h
            for copy in (q_own, q_fwd, p_two, p_one, d_own, d_fwd, r_two, r_one):
                copy(n).wait_send()
        return carry

    lax.fori_loop(0, MID, drain, 0)
    for i in range(2 * MIDS):
        kv_own(i).wait_send()
        kv_back(i).wait_send()
    if nc > 1:
        for x in range(nx):
            core_copy(x).wait_send()
    for k in range(1, nx):
        a_copy(k).wait_send()
        b3_copy(k).wait_send()
    for k in range(1, ny):
        b_copy(k).wait_send()
        a3_copy(k).wait_send()
    for k in range(1, n_ctx):
        f_copy(k).wait_send()
    for out in outs:
        out.wait()


def settle(n, *refs):
    srcs, dsts = refs[:n], refs[n : 2 * n]
    bufs, isem, osem = refs[2 * n : 3 * n], refs[3 * n], refs[3 * n + 1]
    ins = [pltpu.make_async_copy(s, b, isem.at[i]) for i, (s, b) in enumerate(zip(srcs, bufs))]
    outs = [pltpu.make_async_copy(b, d, osem.at[i]) for i, (b, d) in enumerate(zip(bufs, dsts))]
    for copy in ins:
        copy.start()
    for copy, out in zip(ins, outs):
        copy.wait()
        out.start()
    for out in outs:
        out.wait()


def settled(arrays):
    n = len(arrays)
    anyspec = pl.BlockSpec(memory_space=pl.ANY)
    shapes = tuple(jax.ShapeDtypeStruct(a.shape, a.dtype) for a in arrays)
    return pl.pallas_call(
        functools.partial(settle, n),
        out_shape=shapes,
        in_specs=[anyspec] * n,
        out_specs=[anyspec] * n,
        scratch_shapes=[pltpu.VMEM(a.shape, a.dtype) for a in arrays]
        + [pltpu.SemaphoreType.DMA((n,))] * 2,
        compiler_params=pltpu.CompilerParams(vmem_limit_bytes=60 * 1024 * 1024),
    )(*arrays)


def on_device(q, k, v, g, c, w, pb, db, hl, fd):
    n_dp = lax.axis_size("dp")
    n_ctx = lax.axis_size("ctx")
    nx, ny, nc = grid = GRIDS[n_dp]
    rw = 1024 // n_dp
    chunk = (NCH, HALF, HD)
    vm = pltpu.VMEM
    dma = pltpu.SemaphoreType.DMA
    big = jax.ShapeDtypeStruct((1, ROWS, HEADS * HD), BF16)
    anyspec = pl.BlockSpec(memory_space=pl.ANY)
    vmem = pl.BlockSpec(memory_space=pltpu.VMEM)
    smem = pl.BlockSpec(memory_space=pltpu.SMEM)
    wide = vm((ROWS, HEADS * HD), BF16)
    grads = pl.pallas_call(
        functools.partial(kernel, grid, n_ctx),
        out_shape=(big, big, big, big, jax.ShapeDtypeStruct((rw, HD), F32)),
        in_specs=[anyspec] * 6 + [vmem, vmem, smem, smem],
        out_specs=[anyspec] * 4 + [vmem],
        scratch_shapes=[
            wide,
            wide,
            wide,
            wide,
            wide,
            vm((1024, 1024), BF16),
            vm((8, HD), F32),
            vm((HEADS, 7 * HD), F32),
            vm((HEADS, 7, HD, HD), F32),
            vm((2,) + chunk, BF16),
            vm(chunk, F32),
            vm(chunk, F32),
            vm((2,) + chunk, BF16),
            vm((2,) + chunk, BF16),
            vm((4, NCH, HALF, ROWS), BF16),
            vm((4, NCH, HALF, ROWS), F32),
            vm(chunk, F32),
            vm(chunk, F32),
            wide,
            vm(chunk, BF16),
            vm((2,) + chunk, BF16),
            vm(chunk, F32),
            vm(chunk, F32),
            vm((2,) + chunk, BF16),
            vm((2,) + chunk, BF16),
            vm((HEADS, ROWS, HD), F32),
            vm((HEADS, ROWS, HD), F32),
            vm((MIDS, ROWS, HD), BF16),
            vm((MIDS, ROWS, HD), BF16),
            vm((MIDS, ROWS, HD), F32),
            vm((MIDS, ROWS, HD), F32),
            vm((2 * MIDS, ROWS, HD), BF16),
            vm((2 * MIDS, ROWS, HD), BF16),
            vm((2 * MIDS, HALF, HD), BF16),
            vm((2 * MIDS, HALF, HD), BF16),
            wide,
            wide,
            wide,
            wide,
            vm((nc, nx, ny, 2, rw, 512), BF16),
            vm((nx, ny, 2, rw, 512), BF16),
            vm((nx, ny, 2, rw, 512), BF16),
            vm((max(nx - 1, 1), ny, rw, 512), BF16),
            vm((max(ny - 1, 1), nx, rw, 512), BF16),
            vm((ny, rw, 512), BF16),
            vm((nx, rw, 512), BF16),
            vm((max(ny - 1, 1), rw, 512), BF16),
            vm((max(nx - 1, 1), rw, 512), BF16),
            vm((8, rw, HD), BF16),
            vm((7, rw, HD), BF16),
            dma((6,)),
            dma((4,)),
        ]
        + [dma((2, NCH))] * 8
        + [dma((2 * MIDS,))] * 4
        + [dma((4,))] * 10
        + [dma((8,))] * 2
        + [pltpu.SemaphoreType.REGULAR((2,))],
        compiler_params=pltpu.CompilerParams(
            collective_id=0, has_side_effects=True, vmem_limit_bytes=60 * 1024 * 1024
        ),
    )(q, k, v, g, c, w, pb, db, hl, fd)
    return settled(grads)


def solution(mesh):
    rows = P("dp", "ctx", None)
    return jax.shard_map(
        on_device,
        mesh=mesh,
        in_specs=(rows,) * 5 + (P(), P(), P(), P("dp", None), P("dp")),
        out_specs=(rows,) * 4 + (P("dp", "ctx"),),
        check_vma=False,
    )
```

```python
import functools
import math

import jax
import jax.numpy as jnp
from jax import lax
from jax.experimental import pallas as pl
from jax.experimental.pallas import tpu as pltpu
from jax.sharding import PartitionSpec as P

MESH = pl.DeviceIdType.MESH
F32 = jnp.float32
BF16 = jnp.bfloat16
EPS = 1e-05
HEADS = 8
HD = 128
ROWS = 256
HALF = 128
NCH = 16
SCALE = HD ** (-0.5)
GRIDS = {32: (4, 4, 2), 8: (2, 2, 2), 4: (1, 2, 2), 2: (1, 1, 2), 1: (1, 1, 1)}

MID = 4
MIDS = HEADS - MID
PAIRED = MID - MIDS
PER = MID

AHEAD = 4.0
HOP = 3.2
T_OWN = 0.2
T_GATED = 8.95
D_LAG = 1.6
T_CORE = 3.0
T_TWO = 8.0
T_THREE = 10.6
T_FOUR = 13.6


def dot_nn(a, b):
    return lax.dot_general(a, b, (((1,), (0,)), ((), ())), preferred_element_type=F32)


def dot_nt(a, b):
    return lax.dot_general(a, b, (((1,), (1,)), ((), ())), preferred_element_type=F32)


def dot_tn(a, b):
    return lax.dot_general(a, b, (((0,), (0,)), ((), ())), preferred_element_type=F32)


def kernel(
    grid,
    n_ctx,
    q_hbm,
    k_hbm,
    v_hbm,
    g_hbm,
    c_hbm,
    w_hbm,
    pb_ref,
    db_ref,
    hl_ref,
    fd_ref,
    dq_hbm,
    dk_hbm,
    dv_hbm,
    dg_hbm,
    dw_ref,
    q0,
    k0,
    v0,
    g0,
    c0,
    w0,
    idx,
    vtab,
    tb,
    qin,
    p1f,
    mx,
    pout,
    pin,
    asav,
    dsav,
    dgf,
    dnc,
    gt,
    dm0,
    dmin,
    r0f,
    r1f,
    rout,
    rin,
    dka,
    dva,
    kl,
    vl,
    dkl,
    dvl,
    sout,
    sin,
    qmux,
    dmux,
    oq,
    ok,
    ov,
    og,
    wbuf,
    cin,
    c1,
    ain,
    bin_,
    a2,
    b2,
    a3in,
    b3in,
    fbuf,
    fin,
    lsem,
    osem,
    qs,
    qr,
    ps,
    pr,
    ds_,
    dr,
    rs,
    rr,
    ks,
    kr,
    ss,
    sr,
    cs,
    cr,
    as_,
    ar,
    bs,
    br,
    a3s,
    a3r,
    b3s,
    b3r,
    fs,
    fr,
    tell,
):
    nx, ny, nc = grid
    dp = lax.axis_index("dp")
    ctx = lax.axis_index("ctx")
    xi = lax.div(dp, ny * nc)
    yi = lax.rem(lax.div(dp, nc), ny)
    ci = lax.rem(dp, nc)
    left = (dp, lax.rem(ctx + n_ctx - 1, n_ctx))
    right = (dp, lax.rem(ctx + 1, n_ctx))

    def at_x(k):
        return lax.rem(xi + k, nx)

    def at_y(k):
        return lax.rem(yi + k, ny)

    def dev(x, y, c):
        return (x * (ny * nc) + y * nc + c, ctx)

    other = 1 - ci
    peers = [(dp, lax.rem(ctx + k, n_ctx)) for k in sorted({1, n_ctx - 1})]
    peers += [dev(at_x(k), yi, ci) for k in sorted({1, nx - 1} - {0})]
    peers += [dev(xi, at_y(k), ci) for k in sorted({1, ny - 1} - {0})]
    if nc > 1:
        peers.append(dev(xi, yi, other))

    loads = [
        pltpu.make_async_copy(src.at[0] if lead else src, dst, lsem.at[i])
        for i, (src, dst, lead) in enumerate(
            (
                (q_hbm, q0, True),
                (k_hbm, k0, True),
                (v_hbm, v0, True),
                (c_hbm, c0, True),
                (w_hbm, w0, False),
                (g_hbm, g0, True),
            )
        )
    ]
    barrier = pltpu.get_barrier_semaphore()
    for peer in peers:
        pl.semaphore_signal(barrier, inc=1, device_id=peer, device_id_type=MESH)
    for load in loads:
        load.start()

    block = lax.rem(ctx - fd_ref[0] + n_ctx, n_ctx)
    end = jnp.int32(0)
    inner = jnp.int32(0)
    user_len = jnp.int32(0)
    user_blocks = jnp.int32(0)
    for i in range(8):
        length = hl_ref[0, i]
        count = lax.div(length + (ROWS - 1), ROWS)
        start = end
        end = end + count
        inside = (start <= block) & (block < end)
        inner = jnp.where(inside, block - start, inner)
        user_len = jnp.where(inside, length, user_len)
        user_blocks = jnp.where(inside, count, user_blocks)
    live_rows = user_len - inner * ROWS
    valid = [
        None,
        (inner + 1 < user_blocks).astype(jnp.int32).astype(F32),
        (inner + 2 < user_blocks).astype(jnp.int32).astype(F32),
    ]
    second = (inner == 1).astype(jnp.int32).astype(F32)
    third = (inner == 2).astype(jnp.int32).astype(F32)
    not_third = 1.0 - third
    middle = ((inner == 1) & (user_blocks == 3)).astype(jnp.int32).astype(F32)

    def remote(src, dst, ssem, rsem, device):
        return pltpu.make_async_remote_copy(
            src_ref=src,
            dst_ref=dst,
            send_sem=ssem,
            recv_sem=rsem,
            device_id=device,
            device_id_type=MESH,
        )

    def half_of(n):
        return n // HEADS if isinstance(n, int) else lax.div(n, HEADS)

    def head_of(n):
        return n % HEADS if isinstance(n, int) else lax.rem(n, HEADS)

    def rows_of(n):
        r = half_of(n)
        return pl.ds(r * HALF if isinstance(n, int) else pl.multiple_of(r * HALF, HALF), HALF)

    def cols_of(n):
        h = head_of(n)
        return pl.ds(h * HD if isinstance(n, int) else pl.multiple_of(h * HD, HD), HD)

    def q_own(n):
        return remote(q0.at[rows_of(n), cols_of(n)], qin.at[0, n], qs.at[0, n], qr.at[0, n], left)

    def q_fwd(n):
        return remote(qin.at[0, n], qin.at[1, n], qs.at[1, n], qr.at[1, n], left)

    def mux_at(n):
        return half_of(n) * MIDS + head_of(n) - PAIRED

    def q_fwd_paired(n):
        return remote(qmux.at[mux_at(n)], qin.at[1, n], qs.at[1, n], qr.at[1, n], left)

    def d_fwd_paired(n):
        return remote(dmux.at[mux_at(n)], dmin.at[1, n], ds_.at[1, n], dr.at[1, n], left)

    def p_two(n):
        return remote(pout.at[1, n], pin.at[1, n], ps.at[1, n], pr.at[1, n], right)

    def p_one(n):
        return remote(pout.at[0, n], pin.at[0, n], ps.at[0, n], pr.at[0, n], right)

    def d_own(n):
        return remote(dm0.at[n], dmin.at[0, n], ds_.at[0, n], dr.at[0, n], left)

    def d_fwd(n):
        return remote(dmin.at[0, n], dmin.at[1, n], ds_.at[1, n], dr.at[1, n], left)

    def r_two(n):
        return remote(rout.at[1, n], rin.at[1, n], rs.at[1, n], rr.at[1, n], right)

    def r_one(n):
        return remote(rout.at[0, n], rin.at[0, n], rs.at[0, n], rr.at[0, n], right)

    def kv_own(i):
        src, dst = ((k0, kl), (v0, vl))[i % 2]
        h = i // 2
        return remote(
            src.at[:, pl.ds((MID + h) * HD, HD)], dst.at[h], ks.at[i], kr.at[i], right
        )

    def kv_back(i):
        return remote(sout.at[i], sin.at[i], ss.at[i], sr.at[i], left)

    def tables():
        for m in range(6):
            idx[m : m + 1, :] = db_ref[m * HD : (m + 1) * HD].astype(F32).reshape(1, HD)
        idx[6:8, :] = jnp.zeros((2, HD), F32)
        rowi = lax.broadcasted_iota(jnp.int32, (HD, HD), 0)
        coli = lax.broadcasted_iota(jnp.int32, (HD, HD), 1)
        turn = jnp.where(rowi + coli == HD, 1.0, 0.0) + jnp.where(
            (rowi == 0) & (coli == 0), 1.0, 0.0
        )
        turned = dot_nn(idx[...].astype(BF16), turn.astype(BF16))
        lane = lax.broadcasted_iota(jnp.int32, (1, HD), 1)
        bias = pb_ref[...] * 0.5
        hi = bias.astype(BF16)
        rest = bias - hi.astype(F32)
        mid = rest.astype(BF16)
        low = (rest - mid.astype(F32)).astype(BF16)
        for m in range(7):
            before = turned[max(m - 1, 0) : max(m - 1, 0) + 1, :]
            here = turned[m : m + 1, :]
            want = jnp.where(lane == 0, here, before)
            hot = jnp.where(
                rowi.astype(F32) == jnp.broadcast_to(want, (HD, HD)), 1.0, 0.0
            ).astype(BF16)
            vtab[:, m * HD : (m + 1) * HD] = (
                dot_nn(hi, hot) + dot_nn(mid, hot) + dot_nn(low, hot)
            )

        def one_head(h, carry):
            tb[h, 0] = jnp.zeros((HD, HD), F32)
            for m in range(6):
                line = vtab[pl.ds(h, 1), m * HD : (m + 2) * HD]
                wide = jnp.broadcast_to(line, (HD, 2 * HD))
                tb[h, m + 1] = pltpu.roll(wide, 0, 1, stride=1, stride_axis=0)[:, :HD]
            return carry

        lax.fori_loop(0, HEADS, one_head, 0)

    def curve(qc, kh, h, r, o):
        bias = jnp.concatenate([tb[h, 2 * o + r + 1], tb[h, 2 * o + r]], axis=1)
        x = dot_nt(qc, kh) * (0.5 * SCALE) + bias
        th = jnp.tanh(x)
        u = 1.0 + th
        a = x * u
        return a, u + a * (1.0 - th)

    def forward_own(n):
        r, h = half_of(n), head_of(n)
        a, d = curve(q0[rows_of(n), cols_of(n)], k0[:, cols_of(n)], h, r, 0)
        row = lax.broadcasted_iota(jnp.int32, (HALF, ROWS), 0) + r * HALF
        col = lax.broadcasted_iota(jnp.int32, (HALF, ROWS), 1)
        a = jnp.where(col <= row, a, 0.0).astype(BF16)
        asav[0, n] = a
        dsav[0, n] = jnp.where(col <= row, d, 0.0)
        mx[n] = dot_nn(a, v0[:, cols_of(n)])

    def attend(qc, kh, vh, h, r, o, slot, n):
        a, d = curve(qc, kh, h, r, o)
        a = a.astype(BF16)
        asav[slot, n] = a
        dsav[slot, n] = d
        return dot_nn(a, vh)

    def forward(n, paired=False):
        r, h = half_of(n), head_of(n)
        kh, vh = k0[:, cols_of(n)], v0[:, cols_of(n)]
        two = attend(qin[1, n], kh, vh, h, r, 2, 2, n) * valid[2]
        if paired:
            m, hm, i = n + MIDS, h + MIDS, h - PAIRED
            km, vm = k0[:, cols_of(m)], v0[:, cols_of(m)]
            kb, vb = kl[i], vl[i]
            after = attend(qin[1, n], km, vm, hm, r, 1, 1, m)
            after = after + attend(qin[1, n], kb, vb, hm, r, 2, 2, m)
            two = two + after * middle
        pout[1, n] = two.astype(BF16)
        p_two(n).start()
        p1f[n] = attend(qin[0, n], kh, vh, h, r, 1, 1, n) * valid[1]
        if paired:
            mx[m] += attend(q0[rows_of(m), cols_of(m)], kb, vb, hm, r, 1, 3, m) * second

    def masked(x, flag):
        return (x.astype(F32) * flag).astype(BF16)

    def pull(dmc, kh, vh, slot, n):
        dsc = (dot_nt(dmc, vh) * dsav[slot, n]).astype(BF16)
        return dsc, dot_nn(dsc, kh)

    def backward(n, paired=False):
        h = head_of(n)
        kh, vh = k0[:, cols_of(n)], v0[:, cols_of(n)]
        dm_two = masked(dmin[1, n], valid[2])
        ds_two, part = pull(dm_two, kh, vh, 2, n)
        if paired:
            m, hm, i = n + MIDS, h + MIDS, h - PAIRED
            km, vm = k0[:, cols_of(m)], v0[:, cols_of(m)]
            kb, vb = kl[i], vl[i]
            dm_mid = masked(dmin[1, n], middle)
            ds_near, near = pull(dm_mid, km, vm, 1, m)
            ds_far, far = pull(dm_mid, kb, vb, 2, m)
            part = part + near + far
        rout[1, n] = part.astype(BF16)
        r_two(n).start()
        dm_one = masked(dmin[0, n], valid[1])
        ds_one, r1f[n] = pull(dm_one, kh, vh, 1, n)
        ds_own, r0f[n] = pull(dm0[n], kh, vh, 0, n)
        q_own_rows = q0[rows_of(n), cols_of(n)]
        dka[h] += dot_tn(
            jnp.concatenate([ds_two, ds_one, ds_own], axis=0),
            jnp.concatenate([qin[1, n], qin[0, n], q_own_rows], axis=0),
        )
        dva[h] += dot_tn(
            jnp.concatenate([asav[2, n], asav[1, n], asav[0, n]], axis=0),
            jnp.concatenate([dm_two, dm_one, dm0[n]], axis=0),
        )
        if paired:
            qm, qa = q0[rows_of(m), cols_of(m)], qin[1, n]
            dm_back = masked(dm0[m], second)
            ds_back, back = pull(dm_back, kb, vb, 3, m)
            ds_self, own = pull(dm0[m], km, vm, 0, m)
            r0f[m] = own + back
            dka[hm] += dot_tn(
                jnp.concatenate([ds_near, ds_self], axis=0), jnp.concatenate([qa, qm], axis=0)
            )
            dva[hm] += dot_tn(
                jnp.concatenate([asav[1, m], asav[0, m]], axis=0),
                jnp.concatenate([dm_mid, dm0[m]], axis=0),
            )
            dkl[i] += dot_tn(
                jnp.concatenate([ds_far, ds_back], axis=0), jnp.concatenate([qa, qm], axis=0)
            )
            dvl[i] += dot_tn(
                jnp.concatenate([asav[2, m], asav[3, m]], axis=0),
                jnp.concatenate([dm_mid, dm_back], axis=0),
            )

    def mid_out(i):
        sout[2 * i] = (dkl[i] * (0.5 * SCALE)).astype(BF16)
        sout[2 * i + 1] = dvl[i].astype(BF16)
        kv_back(2 * i).start()
        kv_back(2 * i + 1).start()

    def live_mask(r, width):
        row = lax.broadcasted_iota(jnp.int32, (HALF, width), 0) + r * HALF
        return row < live_rows

    def gate_of(r, h):
        return g0[r * HALF : (r + 1) * HALF, h * HD : (h + 1) * HD].astype(F32)

    def d_gated():
        for i in (3, 4, 5):
            loads[i].wait()
        for pair in range(4):
            got = dot_nt(c0[...], w0[pair * 256 : (pair + 1) * 256, :])
            for r in range(2):
                for j in range(2):
                    h = 2 * pair + j
                    dgf[r * HEADS + h] = got[
                        r * HALF : (r + 1) * HALF, j * HD : (j + 1) * HD
                    ]
        for r in range(2):
            mask = live_mask(r, HD)
            total = jnp.zeros((HALF, HD), F32)
            for h in range(HEADS):
                dn = jnp.where(mask, dgf[r * HEADS + h] * gate_of(r, h), 0.0)
                dnc[r * HEADS + h] = dn
                total = total + dn
            mean = jnp.sum(total, axis=1, keepdims=True) * (1.0 / (HEADS * HD))
            for h in range(HEADS):
                dnc[r * HEADS + h] = dnc[r * HEADS + h] - mean

    def norm(r):
        inv_n = 1.0 / (HEADS * HD)
        total = mx[r * HEADS]
        for h in range(1, HEADS):
            total = total + mx[r * HEADS + h]
        mean = jnp.sum(total, axis=1, keepdims=True) * inv_n
        square = jnp.zeros((HALF, HD), F32)
        cross = jnp.zeros((HALF, HD), F32)
        for h in range(HEADS):
            cen = mx[r * HEADS + h] - mean
            mx[r * HEADS + h] = cen
            square = square + cen * cen
            cross = cross + cen * dnc[r * HEADS + h]
        inv = lax.rsqrt(jnp.sum(square, axis=1, keepdims=True) * inv_n + EPS)
        slope = jnp.sum(cross, axis=1, keepdims=True) * inv_n * inv * inv
        for h in range(HEADS):
            n = r * HEADS + h
            dm0[n] = (inv * (dnc[n] - mx[n] * slope)).astype(BF16)

        mask = live_mask(r, HD)
        rows = slice(r * HALF, (r + 1) * HALF)
        for h in range(HEADS):
            n = r * HEADS + h
            cols = slice(h * HD, (h + 1) * HD)
            normed = mx[n] * inv
            gt[rows, cols] = jnp.where(mask, normed * gate_of(r, h), 0.0).astype(BF16)
            og[rows, cols] = jnp.where(mask, dgf[n] * normed, 0.0).astype(BF16)

    rw = 1024 // (nx * ny * nc)

    def core_copy(x):
        return remote(wbuf.at[other, x], cin.at[x], cs.at[x], cr.at[x], dev(xi, yi, other))

    def a_copy(k):
        return remote(
            c1.at[at_x(k), :, 0], ain.at[k - 1], as_.at[k - 1], ar.at[k - 1], dev(at_x(k), yi, ci)
        )

    def b_copy(k):
        return remote(
            c1.at[:, at_y(k), 1], bin_.at[k - 1], bs.at[k - 1], br.at[k - 1], dev(xi, at_y(k), ci)
        )

    def a3_copy(k):
        return remote(
            a2.at[at_y(k)], a3in.at[k - 1], a3s.at[k - 1], a3r.at[k - 1], dev(xi, at_y(k), ci)
        )

    def b3_copy(k):
        return remote(
            b2.at[at_x(k)], b3in.at[k - 1], b3s.at[k - 1], b3r.at[k - 1], dev(at_x(k), yi, ci)
        )

    def f_copy(k):
        to = lax.rem(ctx + k, n_ctx)
        return remote(fbuf.at[to], fin.at[k - 1], fs.at[k - 1], fr.at[k - 1], (dp, to))

    def weight_terms():
        rx = 1024 // nx
        for x in range(nx):
            for half in range(2):
                got = dot_tn(
                    gt[:, x * rx : (x + 1) * rx], c0[:, half * 512 : (half + 1) * 512]
                ).astype(BF16)
                for y in range(ny):
                    for c in range(nc):
                        at = (y * nc + c) * rw
                        wbuf[c, x, y, half] = got[at : at + rw, :]
            if nc > 1:
                core_copy(x).start()

    def after_core():
        for x in range(nx):
            if nc > 1:
                core_copy(x).wait_recv()
            for y in range(ny):
                for half in range(2):
                    got = wbuf[ci, x, y, half].astype(F32)
                    if nc > 1:
                        got = got + cin[x, y, half].astype(F32)
                    c1[x, y, half] = got.astype(BF16)
        if nx == 4:
            pl.semaphore_wait(tell.at[0], 1)
        if ny == 4:
            pl.semaphore_wait(tell.at[1], 1)
        for k in range(1, nx):
            a_copy(k).start()
        for k in range(1, ny):
            b_copy(k).start()

    def after_two():
        for k in range(1, nx):
            a_copy(k).wait_recv()
        for y in range(ny):
            got = c1[xi, y, 0].astype(F32)
            for k in range(1, nx):
                got = got + ain[k - 1, y].astype(F32)
            a2[y] = got.astype(BF16)
        for k in range(1, ny):
            a3_copy(k).start()
        for k in range(1, ny):
            b_copy(k).wait_recv()
        for x in range(nx):
            got = c1[x, yi, 1].astype(F32)
            for k in range(1, ny):
                got = got + bin_[k - 1, x].astype(F32)
            b2[x] = got.astype(BF16)
        for k in range(1, nx):
            b3_copy(k).start()

    def after_three():
        for k in range(1, ny):
            a3_copy(k).wait_recv()
        got = a2[yi].astype(F32)
        for k in range(1, ny):
            got = got + a3in[k - 1].astype(F32)
        for c in range(4):
            fbuf[c] = got[:, c * HD : (c + 1) * HD].astype(BF16)
        for k in range(1, nx):
            b3_copy(k).wait_recv()
        got = b2[xi].astype(F32)
        for k in range(1, nx):
            got = got + b3in[k - 1].astype(F32)
        for c in range(4):
            fbuf[4 + c] = got[:, c * HD : (c + 1) * HD].astype(BF16)
        for k in range(1, n_ctx):
            f_copy(k).start()

    def after_four():
        for k in range(1, n_ctx):
            f_copy(k).wait_recv()
        got = fbuf[ctx].astype(F32)
        for k in range(1, n_ctx):
            got = got + fin[k - 1].astype(F32)
        dw_ref[...] = got

    outs = [
        pltpu.make_async_copy(src, dst.at[0], osem.at[i])
        for i, (src, dst) in enumerate(
            ((oq, dq_hbm), (ok, dk_hbm), (ov, dv_hbm), (og, dg_hbm))
        )
    ]

    def keys_out():
        for h in range(MID):
            cols = slice(h * HD, (h + 1) * HD)
            ok[:, cols] = (dka[h] * (0.5 * SCALE)).astype(BF16)
            ov[:, cols] = dva[h].astype(BF16)

    def mid_in():
        for h in range(MID, HEADS):
            cols = slice(h * HD, (h + 1) * HD)
            i = 2 * (h - MID)
            kv_back(i).wait_recv()
            ok[:, cols] = (dka[h] * (0.5 * SCALE) + sin[i].astype(F32)).astype(BF16)
            kv_back(i + 1).wait_recv()
            ov[:, cols] = (dva[h] + sin[i + 1].astype(F32)).astype(BF16)
        outs[1].start()
        outs[2].start()

    def st_q_own(n):
        q_own(n).start()

    def st_q_fwd(n):
        q_own(n).wait_recv()
        q_fwd(n).start()

    def st_forward(n):
        q_fwd(n).wait_recv()
        forward(n)

    def st_g(n):
        p_two(n).wait_recv()
        pout[0, n] = (p1f[n] + pin[1, n].astype(F32)).astype(BF16)
        p_one(n).start()

    def st_h(n):
        p_one(n).wait_recv()
        mx[n] += pin[0, n].astype(F32)

    def st_d_own(n):
        d_own(n).start()

    def st_d_fwd(n):
        d_own(n).wait_recv()
        d_fwd(n).start()

    def st_backward(n):
        d_fwd(n).wait_recv()
        backward(n)

    def st_c(n):
        r_two(n).wait_recv()
        rout[0, n] = (r1f[n] + rin[1, n].astype(F32)).astype(BF16)
        r_one(n).start()

    def st_e(n):
        r_one(n).wait_recv()
        oq[rows_of(n), cols_of(n)] = (
            (r0f[n] + rin[0, n].astype(F32)) * (0.5 * SCALE)
        ).astype(BF16)

    def either(mine, passing):
        return (mine.astype(F32) * third + passing.astype(F32) * not_third).astype(BF16)

    def st_q_fwd_paired(n):
        m = n + MIDS
        q_own(n).wait_recv()
        qmux[mux_at(n)] = either(q0[rows_of(m), cols_of(m)], qin[0, n])
        q_fwd_paired(n).start()

    def st_d_fwd_paired(n):
        d_own(n).wait_recv()
        dmux[mux_at(n)] = either(dm0[n + MIDS], dmin[0, n])
        d_fwd_paired(n).start()

    def st_forward_paired(n):
        q_fwd(n).wait_recv()
        forward(n, True)

    def st_backward_paired(n):
        d_fwd(n).wait_recv()
        backward(n, True)

    def st_g_paired(n):
        p_two(n).wait_recv()
        got = pin[1, n].astype(F32)
        pout[0, n] = (p1f[n] + got * second).astype(BF16)
        p_one(n).start()
        mx[n + MIDS] += got * third

    def st_c_paired(n):
        r_two(n).wait_recv()
        got = rin[1, n].astype(F32)
        rout[0, n] = (r1f[n] + got * second).astype(BF16)
        r_one(n).start()
        m = n + MIDS
        oq[rows_of(m), cols_of(m)] = ((r0f[m] + got * third) * (0.5 * SCALE)).astype(BF16)

    def kv_wait(i):
        kv_own(2 * i).wait_recv()
        kv_own(2 * i + 1).wait_recv()

    def once(fn):
        return lambda _: fn()

    events = []

    def at(time, fn, n=None):
        events.append((time, fn, n))

    for i in range(2 * MIDS):
        at(max(-AHEAD - 0.1, i // 2 * 2.0 - 3.95), once(kv_own(i).start))
    at(-0.01, once(tables))
    at(T_GATED, once(d_gated))
    first = 0
    for r in range(2):
        base = r * PER
        for h in range(MID):
            n, t, paired = r * HEADS + h, base + h, h >= PAIRED
            at(t - AHEAD, st_q_own, n)
            at(t, st_q_fwd_paired if paired else st_q_fwd, n)
            at(t + T_OWN, forward_own, n)
            if paired:
                at(t + T_OWN, forward_own, n + MIDS)
                if r == 0:
                    at(t + HOP - 0.01, once(functools.partial(kv_wait, h - PAIRED)))
            at(t + HOP, st_forward_paired if paired else st_forward, n)
            at(t + 2 * HOP, st_g_paired if paired else st_g, n)
            at(t + 3 * HOP, st_h, n)
        last_h = max(time for time, fn, n in events if fn is st_h)
        at(last_h + 0.01, once(functools.partial(norm, r)))
        first = max(2 * PER + r * PER, math.ceil(last_h + D_LAG), first + PER)
        turn = list(range(MID))
        if r == 1:
            turn = turn[PAIRED:] + turn[:PAIRED]
        for place, h in enumerate(turn):
            n, t, paired = r * HEADS + h, first + place, h >= PAIRED
            if r == 1 and paired:
                at(t + HOP + 0.02, once(functools.partial(mid_out, h - PAIRED)))
            at(max(t - AHEAD, last_h + 0.02), st_d_own, n)
            at(t, st_d_fwd_paired if paired else st_d_fwd, n)
            at(t + HOP, st_backward_paired if paired else st_backward, n)
            at(t + 2 * HOP, st_c_paired if paired else st_c, n)
            at(t + 3 * HOP, st_e, n)
    end = first + PER
    at(last_h + 0.5, once(weight_terms))
    at(last_h + 0.6, once(outs[3].start))
    at(last_h + T_CORE, once(after_core))
    at(last_h + T_TWO, once(after_two))
    at(last_h + T_THREE, once(after_three))
    at(last_h + T_FOUR, once(after_four))
    at(end - 1 + HOP + 0.03, once(keys_out))
    at(end - 1 + 3 * HOP + 0.1, once(mid_in))

    slots = {}
    for time, fn, n in sorted(events, key=lambda e: e[0]):
        slots.setdefault(math.floor(time), []).append((fn, n))
    order = sorted(slots)

    def steps_of(s):
        return [(fn, None if n is None else n - s) for fn, n in slots[s]]

    dka[...] = jnp.zeros_like(dka)
    dva[...] = jnp.zeros_like(dva)
    dkl[...] = jnp.zeros_like(dkl)
    dvl[...] = jnp.zeros_like(dvl)

    loads[0].wait()
    loads[1].wait()
    loads[2].wait()
    pl.semaphore_wait(barrier, len(peers))
    if nx == 4:
        pl.semaphore_signal(tell.at[0], inc=1, device_id=dev(at_x(3), yi, ci), device_id_type=MESH)
    if ny == 4:
        pl.semaphore_signal(tell.at[1], inc=1, device_id=dev(xi, at_y(3), ci), device_id_type=MESH)
    i = 0
    while i < len(order):
        s = order[i]
        steps = steps_of(s)
        j = i + 1
        while (
            j < len(order)
            and order[j] == s + (j - i)
            and steps_of(order[j]) == steps
            and all(n is not None for _, n in steps)
        ):
            j += 1

        def slot(at_slot, carry, steps=steps):
            for fn, n in steps:
                fn(None if n is None else at_slot + n)
            return carry

        if j - i == 1:
            slot(s, 0)
        else:
            lax.fori_loop(s, s + (j - i), slot, 0)
        i = j
    outs[0].start()

    def drain(h, carry):
        for r in range(2):
            n = r * HEADS + h
            for copy in (q_own, q_fwd, p_two, p_one, d_own, d_fwd, r_two, r_one):
                copy(n).wait_send()
        return carry

    lax.fori_loop(0, MID, drain, 0)
    for i in range(2 * MIDS):
        kv_own(i).wait_send()
        kv_back(i).wait_send()
    if nc > 1:
        for x in range(nx):
            core_copy(x).wait_send()
    for k in range(1, nx):
        a_copy(k).wait_send()
        b3_copy(k).wait_send()
    for k in range(1, ny):
        b_copy(k).wait_send()
        a3_copy(k).wait_send()
    for k in range(1, n_ctx):
        f_copy(k).wait_send()
    for out in outs:
        out.wait()


def settle(n, *refs):
    srcs, dsts = refs[:n], refs[n : 2 * n]
    bufs, isem, osem = refs[2 * n : 3 * n], refs[3 * n], refs[3 * n + 1]
    ins = [pltpu.make_async_copy(s, b, isem.at[i]) for i, (s, b) in enumerate(zip(srcs, bufs))]
    outs = [pltpu.make_async_copy(b, d, osem.at[i]) for i, (b, d) in enumerate(zip(bufs, dsts))]
    for copy in ins:
        copy.start()
    for copy, out in zip(ins, outs):
        copy.wait()
        out.start()
    for out in outs:
        out.wait()


def settled(arrays):
    n = len(arrays)
    anyspec = pl.BlockSpec(memory_space=pl.ANY)
    shapes = tuple(jax.ShapeDtypeStruct(a.shape, a.dtype) for a in arrays)
    return pl.pallas_call(
        functools.partial(settle, n),
        out_shape=shapes,
        in_specs=[anyspec] * n,
        out_specs=[anyspec] * n,
        scratch_shapes=[pltpu.VMEM(a.shape, a.dtype) for a in arrays]
        + [pltpu.SemaphoreType.DMA((n,))] * 2,
        compiler_params=pltpu.CompilerParams(vmem_limit_bytes=60 * 1024 * 1024),
    )(*arrays)


def on_device(q, k, v, g, c, w, pb, db, hl, fd):
    n_dp = lax.axis_size("dp")
    n_ctx = lax.axis_size("ctx")
    nx, ny, nc = grid = GRIDS[n_dp]
    rw = 1024 // n_dp
    chunk = (NCH, HALF, HD)
    vm = pltpu.VMEM
    dma = pltpu.SemaphoreType.DMA
    big = jax.ShapeDtypeStruct((1, ROWS, HEADS * HD), BF16)
    anyspec = pl.BlockSpec(memory_space=pl.ANY)
    vmem = pl.BlockSpec(memory_space=pltpu.VMEM)
    smem = pl.BlockSpec(memory_space=pltpu.SMEM)
    wide = vm((ROWS, HEADS * HD), BF16)
    grads = pl.pallas_call(
        functools.partial(kernel, grid, n_ctx),
        out_shape=(big, big, big, big, jax.ShapeDtypeStruct((rw, HD), F32)),
        in_specs=[anyspec] * 6 + [vmem, vmem, smem, smem],
        out_specs=[anyspec] * 4 + [vmem],
        scratch_shapes=[
            wide,
            wide,
            wide,
            wide,
            wide,
            vm((1024, 1024), BF16),
            vm((8, HD), F32),
            vm((HEADS, 7 * HD), F32),
            vm((HEADS, 7, HD, HD), F32),
            vm((2,) + chunk, BF16),
            vm(chunk, F32),
            vm(chunk, F32),
            vm((2,) + chunk, BF16),
            vm((2,) + chunk, BF16),
            vm((4, NCH, HALF, ROWS), BF16),
            vm((4, NCH, HALF, ROWS), F32),
            vm(chunk, F32),
            vm(chunk, F32),
            wide,
            vm(chunk, BF16),
            vm((2,) + chunk, BF16),
            vm(chunk, F32),
            vm(chunk, F32),
            vm((2,) + chunk, BF16),
            vm((2,) + chunk, BF16),
            vm((HEADS, ROWS, HD), F32),
            vm((HEADS, ROWS, HD), F32),
            vm((MIDS, ROWS, HD), BF16),
            vm((MIDS, ROWS, HD), BF16),
            vm((MIDS, ROWS, HD), F32),
            vm((MIDS, ROWS, HD), F32),
            vm((2 * MIDS, ROWS, HD), BF16),
            vm((2 * MIDS, ROWS, HD), BF16),
            vm((2 * MIDS, HALF, HD), BF16),
            vm((2 * MIDS, HALF, HD), BF16),
            wide,
            wide,
            wide,
            wide,
            vm((nc, nx, ny, 2, rw, 512), BF16),
            vm((nx, ny, 2, rw, 512), BF16),
            vm((nx, ny, 2, rw, 512), BF16),
            vm((max(nx - 1, 1), ny, rw, 512), BF16),
            vm((max(ny - 1, 1), nx, rw, 512), BF16),
            vm((ny, rw, 512), BF16),
            vm((nx, rw, 512), BF16),
            vm((max(ny - 1, 1), rw, 512), BF16),
            vm((max(nx - 1, 1), rw, 512), BF16),
            vm((8, rw, HD), BF16),
            vm((7, rw, HD), BF16),
            dma((6,)),
            dma((4,)),
        ]
        + [dma((2, NCH))] * 8
        + [dma((2 * MIDS,))] * 4
        + [dma((4,))] * 10
        + [dma((8,))] * 2
        + [pltpu.SemaphoreType.REGULAR((2,))],
        compiler_params=pltpu.CompilerParams(
            collective_id=0, has_side_effects=True, vmem_limit_bytes=60 * 1024 * 1024
        ),
    )(q, k, v, g, c, w, pb, db, hl, fd)
    return settled(grads)


def solution(mesh):
    rows = P("dp", "ctx", None)
    return jax.shard_map(
        on_device,
        mesh=mesh,
        in_specs=(rows,) * 5 + (P(), P(), P(), P("dp", None), P("dp")),
        out_specs=(rows,) * 4 + (P("dp", "ctx"),),
        check_vma=False,
    )
```
